128 devices in a mesh: layer: 16 (over y, z), latent: 8 (over x, core).
Axes of the slice: x: 4, y: 4, z: 4, core: 2. Of those that a mesh axis runs over, the one named last changes fastest.
Arguments:
- acts: bfloat16 [1280, 16, 4096], P(None, 'layer'), may hold values from -16 to 16
- active: int32 [1280, 1024], P(None, 'latent'), may hold values 0 or 1
- w_enc: bfloat16 [16, 4096, 1024], P('layer', None, 'latent'), may hold values from -6 to 6
- m_enc: bfloat16 [16, 4096, 1024], P('layer', None, 'latent'), may hold values from -4 to 4
- v_enc: bfloat16 [16, 4096, 1024], P('layer', None, 'latent'), may hold values from 0.0099487305 to 1
- w_dec: bfloat16 [1024, 16, 4096], P('latent', 'layer'), may hold values from -4 to 4
- m_dec: bfloat16 [1024, 16, 4096], P('latent', 'layer'), may hold values from -0.4375 to 0.4375
- v_dec: bfloat16 [1024, 16, 4096], P('latent', 'layer'), may hold values from 9.9658966e-05 to 0.0099487305
Outputs:
- w_enc_new: bfloat16 [16, 4096, 1024], P('layer', None, 'latent')
- m_enc_new: bfloat16 [16, 4096, 1024], P('layer', None, 'latent')
- v_enc_new: bfloat16 [16, 4096, 1024], P('layer', None, 'latent')
- w_dec_new: bfloat16 [1024, 16, 4096], P('latent', 'layer')
- m_dec_new: bfloat16 [1024, 16, 4096], P('latent', 'layer')
- v_dec_new: bfloat16 [1024, 16, 4096], P('latent', 'layer')
The draws below stay inside these ranges and needn't reach their ends.
All inputs are finite; a program needn't handle non-finite values. No bound on the sum of `active` on one device may be relied on, other than what follows from the above.
Results may differ from the reference program's by a relative error of at most 0.02.
Values may be sent and summed in bfloat16 or wider, within the bound.
No kernel may reach another device: no remote copies, remote signals or barrier semaphores. Data moves between devices by JAX's collectives and lax.ppermute only.
A program may use at most 128 MiB of HBM per device.

```python
import math
import jax
import jax.numpy as jnp
from jax import lax

D = 4096
LAT = 1024
TOKENS = 1280
LAYERS = 16


def draw_w_dec(key, part):
    key = jax.random.fold_in(key, 11)
    first_key, second_key = jax.random.split(key)
    position = jnp.arange(LAYERS, dtype=jnp.float32) / max(LAYERS - 1, 1)
    base_draw = jnp.clip(jax.random.normal(first_key, (LAT, LAYERS, D), jnp.float32), -4.0, 4.0)
    growth = 15.0
    factor = jnp.exp(jax.random.uniform(second_key, (LAT,), jnp.float32, jnp.log(0.5), jnp.log(2.0)))
    layer_size = 0.03 * growth ** position
    values = base_draw * layer_size[None, :, None] * factor[:, None, None]
    return jnp.clip(values, -4.0, 4.0).astype(jnp.bfloat16)


def with_ends(values, own_key, smallest, high):
    place = [jax.random.randint(jax.random.fold_in(own_key, axis), (), 0, length) for axis, length in enumerate(values.shape)]
    longest = values.shape.index(max(values.shape))
    next_to = place[:longest] + [(place[longest] + 1) % values.shape[longest]] + place[longest + 1:]
    return values.at[tuple(place)].set(smallest).at[tuple(next_to)].set(high)


def block_levels(rng, dims, pieces, smallest, top_value):
    loudness = 1.0
    for dim, blocks in pieces:
        draws = jax.random.uniform(jax.random.fold_in(jax.random.fold_in(rng, 6), dim), (blocks,), jnp.float32, smallest / len(pieces), top_value / len(pieces))
        loudness = loudness * jnp.repeat(jnp.exp(draws), dims[dim] // blocks).reshape((-1,) + (1,) * (len(dims) - 1 - dim))
    return loudness


def gaussian(own_key, extent, deviation, limit, cuts=(), held_as=jnp.bfloat16):
    values = deviation * jax.random.normal(own_key, extent, jnp.float32)
    if cuts:
        values = values * block_levels(own_key, extent, cuts, -0.22, 0.18)
    return jnp.clip(values, -limit, limit).astype(held_as)


def setup_inputs(seed: int = 0) -> dict:
    key_of = jax.random.split(jax.random.key(seed), 9)
    acts = gaussian(key_of[0], (TOKENS, LAYERS, D), 4.0, 16.0, ((1, 16),))
    active = with_ends((jax.random.randint(key_of[1], (TOKENS, LAT), 0, 4) < 1).astype(jnp.int32), jax.random.fold_in(key_of[1], 1), 0, 1)
    w_enc = gaussian(key_of[2], (LAYERS, D, LAT), 1.0, 6.0, ((0, 16), (2, 8)))
    m_enc = gaussian(key_of[3], (LAYERS, D, LAT), 0.3, 4.0, ((0, 16), (2, 8)))
    v_enc = jnp.clip(jnp.exp(math.log(1.0) - 4.61031033 * jax.random.uniform(key_of[4], (LAYERS, D, LAT), jnp.float32) ** block_levels(key_of[4], (LAYERS, D, LAT), ((0, 16), (2, 8)), -0.2, 0.2)), 0.0099487305, 1.0).astype(jnp.bfloat16)
    w_dec = draw_w_dec(jax.random.fold_in(key_of[8], 71), 0)
    m_dec = gaussian(key_of[6], (LAT, LAYERS, D), 0.03, 0.4375, ((0, 8), (1, 16)))
    v_dec = jnp.clip(jnp.exp(math.log(0.0099487305) - 4.603446 * jax.random.uniform(key_of[7], (LAT, LAYERS, D), jnp.float32) ** block_levels(key_of[7], (LAT, LAYERS, D), ((0, 8), (1, 16)), -0.2, 0.2)), 9.965896606445312e-05, 0.0099487305).astype(jnp.bfloat16)
    return {"acts": acts, "active": active, "w_enc": w_enc, "m_enc": m_enc, "v_enc": v_enc, "w_dec": w_dec, "m_dec": m_dec, "v_dec": v_dec}


def adam_step(weights, gradient, moment_one, moment_two):
    grad_value = gradient.astype(jnp.float32)
    one_new = 0.9 * moment_one.astype(jnp.float32) + 0.1 * grad_value
    two_new = 0.999 * moment_two.astype(jnp.float32) + 0.001 * grad_value * grad_value
    stepped = weights.astype(jnp.float32) - 0.05 * one_new / (jnp.sqrt(two_new) + 1e-08)
    return (stepped, one_new, two_new)

def reference(acts, active, w_enc, m_enc, v_enc, w_dec, m_dec, v_dec):
    enc_scale = (LAYERS * D) ** (-0.5)
    dec_scale = LAT ** (-0.5)
    flat_acts = acts.reshape(TOKENS, LAYERS * D)
    preact = jnp.dot(flat_acts, w_enc.reshape(LAYERS * D, LAT), preferred_element_type=jnp.float32) * enc_scale
    alive_mask = active.astype(jnp.float32)
    latent_codes = (alive_mask * jax.nn.softplus(preact)).astype(jnp.bfloat16)
    dec_flat = w_dec.reshape(LAT, LAYERS * D)
    rebuilt = jnp.dot(latent_codes, dec_flat, preferred_element_type=jnp.float32) * dec_scale
    residue = (rebuilt - flat_acts.astype(jnp.float32)).astype(jnp.bfloat16)
    grad_dec = (lax.dot_general(latent_codes, residue, (((0,), (0,)), ((), ())), preferred_element_type=jnp.float32) * dec_scale).astype(jnp.bfloat16)
    grad_codes = lax.dot_general(residue, dec_flat, (((1,), (1,)), ((), ())), preferred_element_type=jnp.float32) * dec_scale
    grad_pre = (grad_codes * alive_mask * jax.nn.sigmoid(preact)).astype(jnp.bfloat16)
    grad_enc = (lax.dot_general(flat_acts, grad_pre, (((0,), (0,)), ((), ())), preferred_element_type=jnp.float32) * enc_scale).astype(jnp.bfloat16)
    stepped_enc, one_enc, two_enc = adam_step(w_enc, grad_enc.reshape(LAYERS, D, LAT), m_enc, v_enc)
    stepped_dec, one_dec, two_dec = adam_step(w_dec, grad_dec.reshape(LAT, LAYERS, D), m_dec, v_dec)
    layer_rms = jnp.sqrt(lax.optimization_barrier(jnp.mean(stepped_dec * stepped_dec, axis=2)) + 1e-06)
    latent_scale = lax.optimization_barrier(jnp.mean(layer_rms, axis=1))
    w_dec_new = (stepped_dec / latent_scale[:, None, None]).astype(jnp.bfloat16)
    w_enc_new = (stepped_enc * latent_scale[None, None, :]).astype(jnp.bfloat16)
    return (w_enc_new, one_enc.astype(jnp.bfloat16), two_enc.astype(jnp.bfloat16), w_dec_new, one_dec.astype(jnp.bfloat16), two_dec.astype(jnp.bfloat16))
```

```python
import functools

import jax
import jax.numpy as jnp
from jax import lax
from jax.experimental import pallas as pl
from jax.experimental.pallas import tpu as pltpu
from jax.sharding import Mesh
from jax.sharding import PartitionSpec as P

D = 4096
LAT = 1024
TOKENS = 1280
LAYERS = 16
NX = 4
HALF = TOKENS // 2
SHARD = HALF // LAYERS
OWN = 128
WIDE = D // NX
ENC_SCALE = (LAYERS * D) ** (-0.5)
DEC_SCALE = LAT ** (-0.5)
MESSAGE = 48

bf16 = jnp.bfloat16
f32 = jnp.float32


def params(mib=48):
    return pltpu.CompilerParams(vmem_limit_bytes=mib * 1024 * 1024)


def cost(flops, nbytes):
    return pl.CostEstimate(flops=flops, bytes_accessed=nbytes, transcendentals=0)


def adam_step(weights, gradient, moment_one, moment_two):
    one_new = 0.9 * moment_one + 0.1 * gradient
    two_new = 0.999 * moment_two + 0.001 * gradient * gradient
    stepped = weights - 0.05 * one_new / (jnp.sqrt(two_new) + 1e-08)
    return (stepped, one_new, two_new)


def preact_kernel(acts_ref, w_ref, out_ref):
    share = jnp.dot(acts_ref[...], w_ref[...], preferred_element_type=f32)
    out_ref[...] = (share * ENC_SCALE).astype(out_ref.dtype)


def preact_share(acts, w_enc):
    rows = 256
    return pl.pallas_call(
        preact_kernel,
        grid=(TOKENS // rows,),
        in_specs=[
            pl.BlockSpec((rows, D), lambda i: (i, 0)),
            pl.BlockSpec((D, OWN), lambda i: (0, 0)),
        ],
        out_specs=pl.BlockSpec((rows, OWN), lambda i: (i, 0)),
        out_shape=jax.ShapeDtypeStruct((TOKENS, OWN), bf16),
        compiler_params=params(),
        cost_estimate=cost(2 * TOKENS * D * OWN, 2 * TOKENS * D),
        name="preact_share",
    )(acts, w_enc)


def codes_kernel(core_ref, got_ref, alive_ref, codes_ref, slope_ref):
    core = core_ref[0]
    for rel in range(2):
        src = core if rel == 0 else 1 - core
        preact = jnp.sum(got_ref[src].astype(f32), axis=0)
        alive = alive_ref[rel].astype(f32)
        code = (alive * jax.nn.softplus(preact)).astype(bf16)
        codes_ref[:, rel] = jnp.broadcast_to(code[None], (NX * LAYERS, SHARD, OWN))
        slope_ref[rel] = alive * jax.nn.sigmoid(preact)


def make_codes(core, got, alive):
    return pl.pallas_call(
        codes_kernel,
        in_specs=[
            pl.BlockSpec(memory_space=pltpu.SMEM),
            pl.BlockSpec(memory_space=pltpu.VMEM),
            pl.BlockSpec(memory_space=pltpu.VMEM),
        ],
        out_specs=[pl.BlockSpec(memory_space=pltpu.VMEM)] * 2,
        out_shape=[
            jax.ShapeDtypeStruct((NX * LAYERS, 2, SHARD, OWN), bf16),
            jax.ShapeDtypeStruct((2, SHARD, OWN), f32),
        ],
        compiler_params=params(16),
        cost_estimate=cost(1000000, 2000000),
        name="make_codes",
    )(core, got, alive)


def residue_kernel(place_ref, codes_ref, own_ref, other_ref, acts_ref, share_ref, keep_ref, send_ref, flat, cols, wide):
    del place_ref
    weights = (own_ref, other_ref)
    for x in range(NX):
        for rel in range(2):
            part = codes_ref[x * LAYERS:(x + 1) * LAYERS, rel].astype(f32)
            flat[:, (2 * x + rel) * OWN:(2 * x + rel + 1) * OWN] = part.reshape(HALF, OWN).astype(bf16)
            cols[(2 * x + rel) * OWN:(2 * x + rel + 1) * OWN, :] = weights[rel][x]
    rows = 160
    for r in range(HALF // rows):
        rebuilt = jnp.dot(flat[r * rows:(r + 1) * rows, :], cols[...], preferred_element_type=f32) * DEC_SCALE
        wide[r * rows:(r + 1) * rows, :] = (rebuilt - acts_ref[r * rows:(r + 1) * rows, :].astype(f32)).astype(bf16)
    for x in range(NX):
        grad = lax.dot_general(
            wide[...], cols[2 * x * OWN:(2 * x + 2) * OWN, :], (((1,), (1,)), ((), ())), preferred_element_type=f32
        ) * DEC_SCALE
        for rel in range(2):
            share_ref[x * LAYERS:(x + 1) * LAYERS, rel] = (
                grad[:, rel * OWN:(rel + 1) * OWN].reshape(LAYERS, SHARD, OWN).astype(bf16)
            )
    for x in range(NX):
        grad = lax.dot_general(
            flat[:, 2 * x * OWN:(2 * x + 2) * OWN], wide[...], (((0,), (0,)), ((), ())), preferred_element_type=f32
        ) * DEC_SCALE
        keep_ref[x] = grad[:OWN]
        send_ref[x] = grad[OWN:].astype(bf16)


def residue_part(place, codes, own, other, acts):
    whole = lambda *dims: pl.BlockSpec(dims, lambda i, p: (0,) * len(dims))
    return pl.pallas_call(
        residue_kernel,
        grid_spec=pltpu.PrefetchScalarGridSpec(
            num_scalar_prefetch=1,
            grid=(1,),
            in_specs=[
                whole(NX * LAYERS, 2, SHARD, OWN),
                whole(NX, OWN, WIDE),
                whole(NX, OWN, WIDE),
                pl.BlockSpec((HALF, WIDE), lambda i, p: (p[0], p[1])),
            ],
            out_specs=[whole(NX * LAYERS, 2, SHARD, OWN), whole(NX, OWN, WIDE), whole(NX, OWN, WIDE)],
            scratch_shapes=[
                pltpu.VMEM((HALF, LAT), bf16),
                pltpu.VMEM((LAT, WIDE), bf16),
                pltpu.VMEM((HALF, WIDE), bf16),
            ],
        ),
        out_shape=[
            jax.ShapeDtypeStruct((NX * LAYERS, 2, SHARD, OWN), bf16),
            jax.ShapeDtypeStruct((NX, OWN, WIDE), f32),
            jax.ShapeDtypeStruct((NX, OWN, WIDE), bf16),
        ],
        compiler_params=params(),
        cost_estimate=cost(6 * HALF * LAT * WIDE, 10000000),
        name="residue_part",
    )(place, codes, own, other, acts)


def join_kernel(keep_ref, got_ref, out_ref):
    out_ref[...] = (keep_ref[...] + got_ref[...].astype(f32)).astype(bf16)


def join_halves(keep, got):
    block = pl.BlockSpec((1, OWN, WIDE), lambda i: (i, 0, 0))
    return pl.pallas_call(
        join_kernel,
        grid=(NX,),
        in_specs=[block, block],
        out_specs=block,
        out_shape=jax.ShapeDtypeStruct((NX, OWN, WIDE), bf16),
        compiler_params=params(16),
        cost_estimate=cost(1000000, 4000000),
        name="join_halves",
    )(keep, got)


def decoder_kernel(grad_ref, w_ref, m_ref, v_ref, m_out, v_out, stepped_out, rms_out, total):
    step = pl.program_id(0)

    @pl.when(step == 0)
    def _():
        total[...] = jnp.zeros_like(total)

    stepped, one, two = adam_step(
        w_ref[...].astype(f32), grad_ref[0].astype(f32), m_ref[...].astype(f32), v_ref[...].astype(f32)
    )
    m_out[...] = one.astype(bf16)
    v_out[...] = two.astype(bf16)
    stepped_out[...] = stepped
    total[...] += jnp.sum(stepped * stepped, axis=1, keepdims=True)

    @pl.when(step == NX - 1)
    def _():
        rms = jnp.sqrt(total[...] * (1.0 / D) + 1e-06)
        rms_out[...] = jnp.broadcast_to(rms, (OWN, OWN)).T[:8]


def decoder_adam(grad, w, m, v):
    block = pl.BlockSpec((OWN, WIDE), lambda i: (0, i))
    return pl.pallas_call(
        decoder_kernel,
        grid=(NX,),
        in_specs=[pl.BlockSpec((1, OWN, WIDE), lambda i: (i, 0, 0)), block, block, block],
        out_specs=[block, block, block, pl.BlockSpec((8, OWN), lambda i: (0, 0))],
        out_shape=[
            jax.ShapeDtypeStruct((OWN, D), bf16),
            jax.ShapeDtypeStruct((OWN, D), bf16),
            jax.ShapeDtypeStruct((OWN, D), f32),
            jax.ShapeDtypeStruct((8, OWN), f32),
        ],
        scratch_shapes=[pltpu.VMEM((OWN, 1), f32)],
        compiler_params=params(16),
        cost_estimate=cost(20 * OWN * D, 8000000),
        name="decoder_adam",
    )(grad, w, m, v)


def grad_pre_kernel(core_ref, got_ref, slope_ref, rms_ref, out_ref):
    core = core_ref[0]
    rms = rms_ref[...]
    high = rms.astype(bf16).astype(f32)
    mid = (rms - high).astype(bf16).astype(f32)
    low = rms - high - mid
    row = lax.broadcasted_iota(jnp.int32, (8, OWN), 0)
    tail = jnp.where(row == 0, high, jnp.where(row == 1, mid, jnp.where(row == 2, low, 0.0)))
    for rel in range(2):
        grad = jnp.sum(got_ref[:, rel].astype(f32), axis=0) * slope_ref[rel]
        message = jnp.concatenate([grad, tail], axis=0).astype(bf16)
        dest = core if rel == 0 else 1 - core
        out_ref[dest] = jnp.broadcast_to(message[None], (LAYERS, MESSAGE, OWN))


def make_grad_pre(core, got, slope, rms):
    return pl.pallas_call(
        grad_pre_kernel,
        in_specs=[pl.BlockSpec(memory_space=pltpu.SMEM)] + [pl.BlockSpec(memory_space=pltpu.VMEM)] * 3,
        out_specs=pl.BlockSpec(memory_space=pltpu.VMEM),
        out_shape=jax.ShapeDtypeStruct((2, LAYERS, MESSAGE, OWN), bf16),
        compiler_params=params(16),
        cost_estimate=cost(1000000, 2000000),
        name="make_grad_pre",
    )(core, got, slope, rms)


def encoder_kernel(core_ref, got_ref, acts_ref, w_ref, m_ref, v_ref, dec_ref, w_out, m_out, v_out, dec_out, turned, scale):
    @pl.when(pl.program_id(0) == 0)
    def _():
        got = got_ref[...].astype(f32)
        grad_pre = got[:, :, :SHARD].reshape(TOKENS, OWN)
        turned[...] = grad_pre.T.astype(bf16)
        mine = got_ref[core_ref[0]].astype(f32)[:, SHARD:]
        rms = jnp.sum(mine, axis=0)
        scale[...] = jnp.sum(rms[:3], axis=0, keepdims=True) * (1.0 / LAYERS)

    grad = jnp.dot(turned[...], acts_ref[...], preferred_element_type=f32) * ENC_SCALE
    grad = grad.astype(bf16).astype(f32).T
    stepped, one, two = adam_step(w_ref[...].astype(f32), grad, m_ref[...].astype(f32), v_ref[...].astype(f32))
    latent_scale = scale[...]
    w_out[...] = (stepped * latent_scale).astype(bf16)
    m_out[...] = one.astype(bf16)
    v_out[...] = two.astype(bf16)
    column = jnp.broadcast_to(latent_scale, (OWN, OWN)).T[:, :1]
    dec_out[...] = (dec_ref[...] / column).astype(bf16)


def encoder_adam(core, got, acts, w, m, v, stepped_dec):
    width = 512
    block = pl.BlockSpec((width, OWN), lambda i: (i, 0))
    across = pl.BlockSpec((OWN, width), lambda i: (0, i))
    return pl.pallas_call(
        encoder_kernel,
        grid=(D // width,),
        in_specs=[
            pl.BlockSpec(memory_space=pltpu.SMEM),
            pl.BlockSpec((2, LAYERS, MESSAGE, OWN), lambda i: (0, 0, 0, 0)),
            pl.BlockSpec((TOKENS, width), lambda i: (0, i)),
            block,
            block,
            block,
            across,
        ],
        out_specs=[block, block, block, across],
        out_shape=[jax.ShapeDtypeStruct((D, OWN), bf16)] * 3 + [jax.ShapeDtypeStruct((OWN, D), bf16)],
        scratch_shapes=[pltpu.VMEM((OWN, TOKENS), bf16), pltpu.VMEM((1, OWN), f32)],
        compiler_params=params(),
        cost_estimate=cost(2 * TOKENS * D * OWN, 20000000),
        name="encoder_adam",
    )(core, got, acts, w, m, v, stepped_dec)


SWAP = [(0, 1), (1, 0)]
ACROSS = ("x", "y", "z")
TOKEN_AXES = ("core", "y", "z")


def exchange(array, axes):
    flat = array.reshape(-1, array.shape[-1])
    return lax.all_to_all(flat, axes, split_axis=0, concat_axis=0, tiled=True).reshape(array.shape)


def local(acts, active, w_enc, m_enc, v_enc, w_dec, m_dec, v_dec):
    core = lax.axis_index("core")
    layer = lax.axis_index(("y", "z"))
    core_array = core.astype(jnp.int32)[None]
    place = jnp.stack([core, lax.axis_index("x")]).astype(jnp.int32)
    acts = acts[:, 0, :]

    own_cols = exchange(w_dec[:, 0, :].reshape(OWN, NX, WIDE).transpose(1, 0, 2), "x")
    other_cols = lax.ppermute(own_cols, "core", SWAP)

    alive = active.astype(bf16).reshape(2, LAYERS, SHARD, OWN)
    alive = lax.dynamic_index_in_dim(alive, layer, 1, keepdims=False)
    alive_own = lax.dynamic_index_in_dim(alive, core, 0, keepdims=False)
    alive_other = lax.ppermute(lax.dynamic_index_in_dim(alive, 1 - core, 0, keepdims=False), "core", SWAP)
    alive = jnp.stack([alive_own, alive_other])

    share = preact_share(acts, w_enc[0])
    share = exchange(share.reshape(2 * LAYERS, SHARD, OWN), TOKEN_AXES)
    codes, slope = make_codes(core_array, share.reshape(2, LAYERS, SHARD, OWN), alive)
    codes = exchange(codes, ACROSS)
    grad_share, keep, send = residue_part(place, codes, own_cols, other_cols, acts)
    grad_share = exchange(grad_share, ACROSS)

    grad_dec = join_halves(keep, lax.ppermute(send, "core", SWAP))
    grad_dec = exchange(grad_dec, "x")
    m_dec_new, v_dec_new, stepped_dec, rms = decoder_adam(grad_dec, w_dec[:, 0, :], m_dec[:, 0, :], v_dec[:, 0, :])

    messages = exchange(make_grad_pre(core_array, grad_share, slope, rms), TOKEN_AXES)
    w_enc_new, m_enc_new, v_enc_new, w_dec_new = encoder_adam(
        core_array, messages, acts, w_enc[0], m_enc[0], v_enc[0], stepped_dec
    )
    return (
        w_enc_new[None],
        m_enc_new[None],
        v_enc_new[None],
        w_dec_new[:, None, :],
        m_dec_new[:, None, :],
        v_dec_new[:, None, :],
    )


def solution(mesh):
    fine = Mesh(mesh.devices.reshape(4, 4, NX, 2), ("y", "z", "x", "core"))
    layer = ("y", "z")
    latent = ("x", "core")
    return jax.shard_map(
        local,
        mesh=fine,
        in_specs=(
            P(None, layer, None),
            P(None, latent),
            P(layer, None, latent),
            P(layer, None, latent),
            P(layer, None, latent),
            P(latent, layer, None),
            P(latent, layer, None),
            P(latent, layer, None),
        ),
        out_specs=(
            P(layer, None, latent),
            P(layer, None, latent),
            P(layer, None, latent),
            P(latent, layer, None),
            P(latent, layer, None),
            P(latent, layer, None),
        ),
        check_vma=False,
    )
```

```python
import jax
import jax.numpy as jnp
from jax import lax
from jax.experimental import pallas as pl
from jax.experimental.pallas import tpu as pltpu
from jax.sharding import Mesh
from jax.sharding import PartitionSpec as P

D = 4096
LAT = 1024
TOKENS = 1280
LAYERS = 16
NX = 4
HALF = TOKENS // 2
SHARD = HALF // LAYERS
OWN = 128
WIDE = D // NX
ENC_SCALE = (LAYERS * D) ** (-0.5)
DEC_SCALE = LAT ** (-0.5)
MESSAGE = 48

bf16 = jnp.bfloat16
f32 = jnp.float32


def params(mib=48):
    return pltpu.CompilerParams(vmem_limit_bytes=mib * 1024 * 1024)


def cost(flops, nbytes):
    return pl.CostEstimate(flops=flops, bytes_accessed=nbytes, transcendentals=0)


def adam_step(weights, gradient, moment_one, moment_two):
    one_new = 0.9 * moment_one + 0.1 * gradient
    two_new = 0.999 * moment_two + 0.001 * gradient * gradient
    stepped = weights - 0.05 * one_new / (jnp.sqrt(two_new) + 1e-08)
    return (stepped, one_new, two_new)


CHUNKS = 8
CHUNK = TOKENS // CHUNKS


def preact_kernel(acts_ref, w_ref, dec_ref, out_ref, *rest):
    pieces, (rows, weights, dec, row_sems, weight_sem, cut_sems) = rest[:NX], rest[NX:]
    here = lax.axis_index("x")
    fetch = pltpu.make_async_copy(w_ref, weights, weight_sem)
    fetch.start()

    def block(c):
        source = acts_ref.at[pl.ds(pl.multiple_of(c * CHUNK, CHUNK), CHUNK)]
        return pltpu.make_async_copy(source, rows.at[c], row_sems.at[c])

    block(0).start()
    block(1).start()
    cuts = []
    for r in range(NX):
        start = pl.multiple_of(lax.rem(here + r, NX) * WIDE, WIDE)
        cuts.append((
            pltpu.make_async_copy(dec_ref.at[:, pl.ds(start, WIDE)], dec.at[r], cut_sems.at[0, r]),
            pltpu.make_async_copy(dec.at[r], pieces[r], cut_sems.at[1, r]),
        ))
        cuts[r][0].start()

    @pl.loop(2, CHUNKS)
    def _(c):
        block(c).start()

    def multiply(c):
        block(c).wait()
        share = jnp.dot(rows[c], weights[...], preferred_element_type=f32)
        out_ref[pl.ds(pl.multiple_of(c * CHUNK, CHUNK), CHUNK), :] = (share * ENC_SCALE).astype(out_ref.dtype)

    fetch.wait()

    @pl.loop(0, CHUNKS // 2)
    def _(c):
        multiply(c)

    for take, give in cuts:
        take.wait()
        give.start()

    @pl.loop(CHUNKS // 2, CHUNKS)
    def _(c):
        multiply(c)

    for _, give in cuts:
        give.wait()


def preact_share(acts, w_enc, w_dec):
    anywhere = pl.BlockSpec(memory_space=pl.ANY)
    return pl.pallas_call(
        preact_kernel,
        in_specs=[anywhere] * 3,
        out_specs=[pl.BlockSpec(memory_space=pltpu.VMEM)] + [anywhere] * NX,
        out_shape=[jax.ShapeDtypeStruct((TOKENS, OWN), bf16)] + [jax.ShapeDtypeStruct((OWN, WIDE), bf16)] * NX,
        scratch_shapes=[
            pltpu.VMEM((CHUNKS, CHUNK, D), bf16),
            pltpu.VMEM((D, OWN), bf16),
            pltpu.VMEM((NX, OWN, WIDE), bf16),
            pltpu.SemaphoreType.DMA((CHUNKS,)),
            pltpu.SemaphoreType.DMA,
            pltpu.SemaphoreType.DMA((2, NX)),
        ],
        compiler_params=params(60),
        cost_estimate=cost(2 * TOKENS * D * OWN, 2 * TOKENS * D),
        name="preact_share",
    )(acts, w_enc, w_dec)


def codes_kernel(place_ref, got_ref, alive_ref, codes_ref, slope_ref):
    core = place_ref[0]
    codes = []
    for rel in range(2):
        src = core if rel == 0 else 1 - core
        preact = jnp.sum(got_ref[src].astype(f32), axis=0)
        alive = alive_ref[rel].astype(f32)
        codes.append(alive * jax.nn.softplus(preact))
        slope_ref[rel] = alive * jax.nn.sigmoid(preact)
    codes_ref[...] = jnp.concatenate(codes, axis=0).astype(bf16)


def make_codes(place, got, alive):
    held = pl.BlockSpec(memory_space=pltpu.VMEM)
    return pl.pallas_call(
        codes_kernel,
        in_specs=[pl.BlockSpec(memory_space=pltpu.SMEM), held, held],
        out_specs=[held] * 2,
        out_shape=[
            jax.ShapeDtypeStruct((2 * SHARD, OWN), bf16),
            jax.ShapeDtypeStruct((2, SHARD, OWN), f32),
        ],
        compiler_params=params(16),
        cost_estimate=cost(1000000, 2000000),
        name="make_codes",
    )(place, got, alive)


def spread_kernel(*refs):
    out_ref = refs[NX]
    for r in range(NX):
        out_ref[:, r] = jnp.broadcast_to(refs[r][...][None], (LAYERS, 2 * SHARD, OWN))


def spread_codes(parts):
    held = pl.BlockSpec(memory_space=pltpu.VMEM)
    return pl.pallas_call(
        spread_kernel,
        in_specs=[held] * NX,
        out_specs=held,
        out_shape=jax.ShapeDtypeStruct((LAYERS, NX, 2 * SHARD, OWN), bf16),
        compiler_params=params(16),
        cost_estimate=cost(1000000, 2000000),
        name="spread_codes",
    )(*parts)


ROWS = 160


def residue_kernel(place_ref, codes_ref, acts_ref, *rest):
    pieces, rest = rest[:2 * NX], rest[2 * NX:]
    share_ref, wide_ref, own_ref, other_ref, got, own_acts, flat, cols, wide, share, in_sems, out_sems = rest
    here = place_ref[1]
    fetch_codes, fetch_cols = [], []
    for r in range(NX):
        fetch_codes.append(pltpu.make_async_copy(codes_ref.at[:, r], got.at[r], in_sems.at[r]))
        for rel in range(2):
            fetch_cols.append(
                pltpu.make_async_copy(
                    pieces[NX * rel + r], cols.at[rel, pl.ds(r * OWN, OWN)], in_sems.at[NX + 2 * r + rel]
                )
            )
    tokens = pl.ds(pl.multiple_of(place_ref[0] * HALF, HALF), HALF)
    width = pl.ds(pl.multiple_of(here * WIDE, WIDE), WIDE)
    fetch_acts = pltpu.make_async_copy(acts_ref.at[tokens, width], own_acts, in_sems.at[3 * NX])
    for copy in fetch_codes + fetch_cols + [fetch_acts]:
        copy.start()
    for r in range(NX):
        fetch_codes[r].wait()
        part = got[r].astype(f32)
        for rel in range(2):
            half = part[:, rel * SHARD:(rel + 1) * SHARD].reshape(HALF, OWN).astype(bf16)
            flat[rel, :, r * OWN:(r + 1) * OWN] = half
    stores = [
        pltpu.make_async_copy(flat.at[0], own_ref, out_sems.at[0]),
        pltpu.make_async_copy(flat.at[1], other_ref, out_sems.at[1]),
        pltpu.make_async_copy(wide, wide_ref, out_sems.at[2]),
        pltpu.make_async_copy(share, share_ref, out_sems.at[3]),
    ]
    stores[0].start()
    stores[1].start()
    for copy in fetch_cols + [fetch_acts]:
        copy.wait()
    for c in range(HALF // ROWS):
        rows = slice(c * ROWS, (c + 1) * ROWS)
        rebuilt = jnp.dot(flat[0, rows, :], cols[0], preferred_element_type=f32)
        rebuilt += jnp.dot(flat[1, rows, :], cols[1], preferred_element_type=f32)
        wide[rows, :] = (rebuilt * DEC_SCALE - own_acts[rows, :].astype(f32)).astype(bf16)
    stores[2].start()
    for pair in range(NX // 2):
        span = slice(2 * pair * OWN, 2 * (pair + 1) * OWN)
        grads = [
            lax.dot_general(
                wide[...], cols[rel, span, :], (((1,), (1,)), ((), ())), preferred_element_type=f32
            ) * DEC_SCALE
            for rel in range(2)
        ]
        for i in range(2):
            parts = [grads[rel][:, i * OWN:(i + 1) * OWN].reshape(LAYERS, SHARD, OWN) for rel in range(2)]
            share[:, 2 * pair + i] = jnp.concatenate(parts, axis=1).astype(bf16)
    stores[3].start()
    for copy in stores:
        copy.wait()


def residue_part(place, codes, acts, pieces):
    anywhere = pl.BlockSpec(memory_space=pl.ANY)
    return pl.pallas_call(
        residue_kernel,
        in_specs=[pl.BlockSpec(memory_space=pltpu.SMEM)] + [anywhere] * (2 + 2 * NX),
        out_specs=[anywhere] * 4,
        scratch_shapes=[
            pltpu.VMEM((NX, LAYERS, 2 * SHARD, OWN), bf16),
            pltpu.VMEM((HALF, WIDE), bf16),
            pltpu.VMEM((2, HALF, NX * OWN), bf16),
            pltpu.VMEM((2, NX * OWN, WIDE), bf16),
            pltpu.VMEM((HALF, WIDE), bf16),
            pltpu.VMEM((LAYERS, NX, 2 * SHARD, OWN), bf16),
            pltpu.SemaphoreType.DMA((3 * NX + 1,)),
            pltpu.SemaphoreType.DMA((4,)),
        ],
        out_shape=[
            jax.ShapeDtypeStruct((LAYERS, NX, 2 * SHARD, OWN), bf16),
            jax.ShapeDtypeStruct((HALF, WIDE), bf16),
            jax.ShapeDtypeStruct((HALF, NX * OWN), bf16),
            jax.ShapeDtypeStruct((HALF, NX * OWN), bf16),
        ],
        compiler_params=params(60),
        cost_estimate=cost(4 * HALF * LAT * WIDE, 10000000),
        name="residue_part",
    )(place, codes, acts, *pieces)


def gradient_kernel(own_ref, wide_ref, own_got_ref, wide_got_ref, *rest):
    outs, (codes, wide, grads, in_sems, out_sems) = rest[:NX], rest[NX:]
    fetches = []
    for i, (left, right) in enumerate(((own_ref, wide_ref), (own_got_ref, wide_got_ref))):
        rows = pl.ds(i * HALF, HALF)
        fetches.append(pltpu.make_async_copy(left, codes.at[rows], in_sems.at[2 * i]))
        fetches.append(pltpu.make_async_copy(right, wide.at[rows], in_sems.at[2 * i + 1]))
    for copy in fetches:
        copy.start()
    for copy in fetches:
        copy.wait()
    stores = []
    for pair in range(NX // 2):
        span = slice(2 * pair * OWN, 2 * (pair + 1) * OWN)
        grad = lax.dot_general(
            codes[:, span], wide[...], (((0,), (0,)), ((), ())), preferred_element_type=f32
        ) * DEC_SCALE
        for i in range(2):
            r = 2 * pair + i
            grads[r] = grad[i * OWN:(i + 1) * OWN].astype(bf16)
            stores.append(pltpu.make_async_copy(grads.at[r], outs[r], out_sems.at[r]))
            stores[r].start()
    for copy in stores:
        copy.wait()


def decoder_gradient(own, wide, own_got, wide_got):
    anywhere = pl.BlockSpec(memory_space=pl.ANY)
    return pl.pallas_call(
        gradient_kernel,
        in_specs=[anywhere] * 4,
        out_specs=[anywhere] * NX,
        out_shape=[jax.ShapeDtypeStruct((OWN, WIDE), bf16)] * NX,
        scratch_shapes=[
            pltpu.VMEM((TOKENS, NX * OWN), bf16),
            pltpu.VMEM((TOKENS, WIDE), bf16),
            pltpu.VMEM((NX, OWN, WIDE), bf16),
            pltpu.SemaphoreType.DMA((4,)),
            pltpu.SemaphoreType.DMA((NX,)),
        ],
        compiler_params=params(60),
        cost_estimate=cost(2 * HALF * LAT * WIDE, 5000000),
        name="decoder_gradient",
    )(own, wide, own_got, wide_got)


def decoder_kernel(place_ref, *refs):
    grads, refs = refs[:NX], refs[NX:]
    w_ref, m_ref, v_ref, m_out, v_out, stepped_out, rms_out, taken, moved, held, in_sems, out_sems = refs
    fetches, stores = [], []
    for r in range(NX):
        span = pl.ds(pl.multiple_of(lax.rem(place_ref[1] + r, NX) * WIDE, WIDE), WIDE)
        sources = (grads[r], w_ref.at[:, span], m_ref.at[:, span], v_ref.at[:, span])
        fetches.append([
            pltpu.make_async_copy(source, taken.at[r, i], in_sems.at[r, i]) for i, source in enumerate(sources)
        ])
        stores.append([
            pltpu.make_async_copy(moved.at[r, 0], m_out.at[:, span], out_sems.at[r, 0]),
            pltpu.make_async_copy(moved.at[r, 1], v_out.at[:, span], out_sems.at[r, 1]),
            pltpu.make_async_copy(held.at[r], stepped_out.at[:, span], out_sems.at[r, 2]),
        ])
    for copies in fetches:
        for copy in copies:
            copy.start()
    total = jnp.zeros((OWN, 1), f32)
    for r in range(NX):
        for copy in fetches[r]:
            copy.wait()
        grad, w, m, v = (taken[r, i].astype(f32) for i in range(4))
        stepped, one, two = adam_step(w, grad, m, v)
        moved[r, 0] = one.astype(bf16)
        moved[r, 1] = two.astype(bf16)
        held[r] = stepped
        for copy in stores[r]:
            copy.start()
        total += jnp.sum(stepped * stepped, axis=1, keepdims=True)
    rms = jnp.sqrt(total * (1.0 / D) + 1e-06)
    rms_out[...] = jnp.broadcast_to(rms, (OWN, OWN)).T[:8]
    for copies in stores:
        for copy in copies:
            copy.wait()


def decoder_adam(place, grads, w, m, v):
    anywhere = pl.BlockSpec(memory_space=pl.ANY)
    return pl.pallas_call(
        decoder_kernel,
        in_specs=[pl.BlockSpec(memory_space=pltpu.SMEM)] + [anywhere] * (NX + 3),
        out_specs=[anywhere] * 3 + [pl.BlockSpec(memory_space=pltpu.VMEM)],
        out_shape=[
            jax.ShapeDtypeStruct((OWN, D), bf16),
            jax.ShapeDtypeStruct((OWN, D), bf16),
            jax.ShapeDtypeStruct((OWN, D), f32),
            jax.ShapeDtypeStruct((8, OWN), f32),
        ],
        scratch_shapes=[
            pltpu.VMEM((NX, 4, OWN, WIDE), bf16),
            pltpu.VMEM((NX, 2, OWN, WIDE), bf16),
            pltpu.VMEM((NX, OWN, WIDE), f32),
            pltpu.SemaphoreType.DMA((NX, 4)),
            pltpu.SemaphoreType.DMA((NX, 3)),
        ],
        compiler_params=params(60),
        cost_estimate=cost(20 * OWN * D, 8000000),
        name="decoder_adam",
    )(place, *grads, w, m, v)


def sum_kernel(got_ref, keep_ref, *outs):
    for r in range(NX):
        both = jnp.sum(got_ref[:, r].astype(f32), axis=0)
        for rel in range(2):
            total = both[rel * SHARD:(rel + 1) * SHARD]
            if r == 0:
                keep_ref[rel] = total
            else:
                outs[r - 1][rel] = total.astype(bf16)


def sum_layers(got):
    return pl.pallas_call(
        sum_kernel,
        in_specs=[pl.BlockSpec(memory_space=pltpu.VMEM)],
        out_specs=[pl.BlockSpec(memory_space=pltpu.VMEM)] * NX,
        out_shape=[jax.ShapeDtypeStruct((2, SHARD, OWN), f32)]
        + [jax.ShapeDtypeStruct((2, SHARD, OWN), bf16)] * (NX - 1),
        compiler_params=params(16),
        cost_estimate=cost(1000000, 2000000),
        name="sum_layers",
    )(got)


def grad_pre_kernel(core_ref, keep_ref, one_ref, two_ref, three_ref, slope_ref, rms_ref, out_ref):
    core = core_ref[0]
    rms = rms_ref[...]
    high = rms.astype(bf16).astype(f32)
    mid = (rms - high).astype(bf16).astype(f32)
    low = rms - high - mid
    row = lax.broadcasted_iota(jnp.int32, (8, OWN), 0)
    tail = jnp.where(row == 0, high, jnp.where(row == 1, mid, jnp.where(row == 2, low, 0.0)))
    for rel in range(2):
        grad = keep_ref[rel] + one_ref[rel].astype(f32) + two_ref[rel].astype(f32) + three_ref[rel].astype(f32)
        message = jnp.concatenate([grad * slope_ref[rel], tail], axis=0).astype(bf16)
        dest = core if rel == 0 else 1 - core
        out_ref[dest] = jnp.broadcast_to(message[None], (LAYERS, MESSAGE, OWN))


def make_grad_pre(core, parts, slope, rms):
    return pl.pallas_call(
        grad_pre_kernel,
        in_specs=[pl.BlockSpec(memory_space=pltpu.SMEM)] + [pl.BlockSpec(memory_space=pltpu.VMEM)] * 6,
        out_specs=pl.BlockSpec(memory_space=pltpu.VMEM),
        out_shape=jax.ShapeDtypeStruct((2, LAYERS, MESSAGE, OWN), bf16),
        compiler_params=params(16),
        cost_estimate=cost(1000000, 2000000),
        name="make_grad_pre",
    )(core, *parts, slope, rms)


PART = 1024
PARTS = D // PART


def encoder_kernel(core_ref, got_ref, w_ref, m_ref, v_ref, acts_ref, dec_ref, *rest):
    w_out, m_out, v_out, dec_out, acts, dec, w_new, m_new, v_new, dec_new, turned, in_sems, out_sems = rest

    def span(c):
        return pl.ds(pl.multiple_of(c * PART, PART), PART)

    def fetches(c):
        return (
            pltpu.make_async_copy(acts_ref.at[:, span(c)], acts.at[c], in_sems.at[c, 0]),
            pltpu.make_async_copy(dec_ref.at[:, span(c)], dec.at[c], in_sems.at[c, 1]),
        )

    def stores(c):
        return (
            pltpu.make_async_copy(w_new.at[c], w_out.at[span(c)], out_sems.at[c, 0]),
            pltpu.make_async_copy(m_new.at[c], m_out.at[span(c)], out_sems.at[c, 1]),
            pltpu.make_async_copy(v_new.at[c], v_out.at[span(c)], out_sems.at[c, 2]),
            pltpu.make_async_copy(dec_new.at[c], dec_out.at[:, span(c)], out_sems.at[c, 3]),
        )

    @pl.loop(0, PARTS)
    def _(c):
        for copy in fetches(c):
            copy.start()

    got = got_ref[...].astype(f32)
    turned[...] = got[:, :, :SHARD].reshape(TOKENS, OWN).T.astype(bf16)
    rms = jnp.sum(got_ref[core_ref[0]].astype(f32)[:, SHARD:], axis=0)
    row = jnp.sum(rms[:3], axis=0, keepdims=True) * (1.0 / LAYERS)
    column = jnp.broadcast_to(row, (OWN, OWN)).T[:, :1]

    @pl.loop(0, PARTS)
    def _(c):
        for copy in fetches(c):
            copy.wait()
        grad = jnp.dot(turned[...], acts[c], preferred_element_type=f32) * ENC_SCALE
        grad = grad.astype(bf16).astype(f32).T
        stepped, one, two = adam_step(
            w_ref[span(c), :].astype(f32), grad, m_ref[span(c), :].astype(f32), v_ref[span(c), :].astype(f32)
        )
        w_new[c] = (stepped * row).astype(bf16)
        m_new[c] = one.astype(bf16)
        v_new[c] = two.astype(bf16)
        dec_new[c] = (dec[c] / column).astype(bf16)
        for copy in stores(c):
            copy.start()

    @pl.loop(0, PARTS)
    def _(c):
        for copy in stores(c):
            copy.wait()


def encoder_adam(core, got, acts, w, m, v, stepped_dec):
    held = pl.BlockSpec(memory_space=pltpu.VMEM)
    anywhere = pl.BlockSpec(memory_space=pl.ANY)
    return pl.pallas_call(
        encoder_kernel,
        in_specs=[pl.BlockSpec(memory_space=pltpu.SMEM)] + [held] * 4 + [anywhere] * 2,
        out_specs=[anywhere] * 4,
        out_shape=[jax.ShapeDtypeStruct((D, OWN), bf16)] * 3 + [jax.ShapeDtypeStruct((OWN, D), bf16)],
        scratch_shapes=[
            pltpu.VMEM((PARTS, TOKENS, PART), bf16),
            pltpu.VMEM((PARTS, OWN, PART), f32),
            pltpu.VMEM((PARTS, PART, OWN), bf16),
            pltpu.VMEM((PARTS, PART, OWN), bf16),
            pltpu.VMEM((PARTS, PART, OWN), bf16),
            pltpu.VMEM((PARTS, OWN, PART), bf16),
            pltpu.VMEM((OWN, TOKENS), bf16),
            pltpu.SemaphoreType.DMA((PARTS, 2)),
            pltpu.SemaphoreType.DMA((PARTS, 4)),
        ],
        compiler_params=params(52),
        cost_estimate=cost(2 * TOKENS * D * OWN, 20000000),
        name="encoder_adam",
    )(core, got, w, m, v, acts, stepped_dec)


def swap(array):
    return lax.ppermute(array, "core", [(0, 1), (1, 0)])


def shift(array, steps):
    return lax.ppermute(array, "x", [(i, (i + steps) % NX) for i in range(NX)])


def exchange(array, axes):
    flat = array.reshape(-1, array.shape[-1])
    return lax.all_to_all(flat, axes, split_axis=0, concat_axis=0, tiled=True).reshape(array.shape)


LAYER_AXES = ("y", "z")
TOKEN_AXES = ("core", "y", "z")


def local(acts, active, w_enc, m_enc, v_enc, w_dec, m_dec, v_dec):
    core = lax.axis_index("core")
    layer = lax.axis_index(LAYER_AXES)
    place = jnp.stack([core, lax.axis_index("x")]).astype(jnp.int32)
    acts, w_dec, m_dec, v_dec = (array[:, 0, :] for array in (acts, w_dec, m_dec, v_dec))

    alive = active.astype(bf16).reshape(2, LAYERS, SHARD, OWN)
    alive = lax.dynamic_index_in_dim(alive, layer, 1, keepdims=False)
    alive_own = lax.dynamic_index_in_dim(alive, core, 0, keepdims=False)
    alive_other = swap(lax.dynamic_index_in_dim(alive, 1 - core, 0, keepdims=False))
    alive = jnp.stack([alive_own, alive_other])

    share, *mine = preact_share(acts, w_enc[0], w_dec)
    own_cols = [mine[0]] + [shift(mine[r], r) for r in range(1, NX)]
    share = exchange(share.reshape(2, LAYERS, SHARD, OWN), TOKEN_AXES)
    codes, slope = make_codes(place, share, alive)
    codes = spread_codes([codes] + [shift(codes, r) for r in range(1, NX)])
    codes = exchange(codes, LAYER_AXES)
    other_cols = [swap(piece) for piece in own_cols]
    grad_share, wide, own, other = residue_part(place, codes, acts, own_cols + other_cols)
    grad_share = exchange(grad_share, LAYER_AXES)

    grad_dec = decoder_gradient(own, wide, swap(other), swap(wide))
    grad_dec = [grad_dec[0]] + [shift(grad_dec[r], NX - r) for r in range(1, NX)]
    m_dec_new, v_dec_new, stepped_dec, rms = decoder_adam(place, grad_dec, w_dec, m_dec, v_dec)

    parts = sum_layers(grad_share)
    parts = [parts[0]] + [shift(parts[r], NX - r) for r in range(1, NX)]
    messages = exchange(make_grad_pre(place, parts, slope, rms), TOKEN_AXES)
    w_enc_new, m_enc_new, v_enc_new, w_dec_new = encoder_adam(
        place, messages, acts, w_enc[0], m_enc[0], v_enc[0], stepped_dec
    )
    return (
        w_enc_new[None],
        m_enc_new[None],
        v_enc_new[None],
        w_dec_new[:, None, :],
        m_dec_new[:, None, :],
        v_dec_new[:, None, :],
    )


def solution(mesh):
    fine = Mesh(mesh.devices.reshape(4, 4, NX, 2), ("y", "z", "x", "core"))
    layer = ("y", "z")
    latent = ("x", "core")
    return jax.shard_map(
        local,
        mesh=fine,
        in_specs=(
            P(None, layer, None),
            P(None, latent),
            P(layer, None, latent),
            P(layer, None, latent),
            P(layer, None, latent),
            P(latent, layer, None),
            P(latent, layer, None),
            P(latent, layer, None),
        ),
        out_specs=(
            P(layer, None, latent),
            P(layer, None, latent),
            P(layer, None, latent),
            P(latent, layer, None),
            P(latent, layer, None),
            P(latent, layer, None),
        ),
        check_vma=False,
    )
```

```python
import jax
import jax.numpy as jnp
from jax import lax
from jax.experimental import pallas as pl
from jax.experimental.pallas import tpu as pltpu
from jax.sharding import Mesh
from jax.sharding import PartitionSpec as P

D = 4096
LAT = 1024
TOKENS = 1280
LAYERS = 16
NX = 4
HALF = TOKENS // 2
SHARD = HALF // LAYERS
OWN = 128
WIDE = D // NX
ENC_SCALE = (LAYERS * D) ** (-0.5)
DEC_SCALE = LAT ** (-0.5)
MESSAGE = 48

bf16 = jnp.bfloat16
f32 = jnp.float32


def params(mib=48):
    return pltpu.CompilerParams(vmem_limit_bytes=mib * 1024 * 1024)


def cost(flops, nbytes):
    return pl.CostEstimate(flops=flops, bytes_accessed=nbytes, transcendentals=0)


def adam_step(weights, gradient, moment_one, moment_two):
    one_new = 0.9 * moment_one + 0.1 * gradient
    two_new = 0.999 * moment_two + 0.001 * gradient * gradient
    stepped = weights - 0.05 * one_new / (jnp.sqrt(two_new) + 1e-08)
    return (stepped, one_new, two_new)


CHUNKS = 8
CHUNK = TOKENS // CHUNKS


def preact_kernel(acts_ref, w_ref, dec_ref, out_ref, *rest):
    pieces, (rows, weights, dec, row_sems, weight_sem, cut_sems) = rest[:NX], rest[NX:]
    here = lax.axis_index("x")
    fetch = pltpu.make_async_copy(w_ref, weights, weight_sem)
    fetch.start()

    def block(c):
        source = acts_ref.at[pl.ds(pl.multiple_of(c * CHUNK, CHUNK), CHUNK)]
        return pltpu.make_async_copy(source, rows.at[c], row_sems.at[c])

    block(0).start()
    block(1).start()
    cuts = []
    for r in range(NX):
        start = pl.multiple_of(lax.rem(here + r, NX) * WIDE, WIDE)
        cuts.append((
            pltpu.make_async_copy(dec_ref.at[:, pl.ds(start, WIDE)], dec.at[r], cut_sems.at[0, r]),
            pltpu.make_async_copy(dec.at[r], pieces[r], cut_sems.at[1, r]),
        ))
        cuts[r][0].start()

    @pl.loop(2, CHUNKS)
    def _(c):
        block(c).start()

    def multiply(c):
        block(c).wait()
        share = jnp.dot(rows[c], weights[...], preferred_element_type=f32)
        out_ref[pl.ds(pl.multiple_of(c * CHUNK, CHUNK), CHUNK), :] = (share * ENC_SCALE).astype(out_ref.dtype)

    fetch.wait()

    @pl.loop(0, CHUNKS // 2)
    def _(c):
        multiply(c)

    for take, give in cuts:
        take.wait()
        give.start()

    @pl.loop(CHUNKS // 2, CHUNKS)
    def _(c):
        multiply(c)

    for _, give in cuts:
        give.wait()


def preact_share(acts, w_enc, w_dec):
    anywhere = pl.BlockSpec(memory_space=pl.ANY)
    return pl.pallas_call(
        preact_kernel,
        in_specs=[anywhere] * 3,
        out_specs=[pl.BlockSpec(memory_space=pltpu.VMEM)] + [anywhere] * NX,
        out_shape=[jax.ShapeDtypeStruct((TOKENS, OWN), bf16)] + [jax.ShapeDtypeStruct((OWN, WIDE), bf16)] * NX,
        scratch_shapes=[
            pltpu.VMEM((CHUNKS, CHUNK, D), bf16),
            pltpu.VMEM((D, OWN), bf16),
            pltpu.VMEM((NX, OWN, WIDE), bf16),
            pltpu.SemaphoreType.DMA((CHUNKS,)),
            pltpu.SemaphoreType.DMA,
            pltpu.SemaphoreType.DMA((2, NX)),
        ],
        compiler_params=params(60),
        cost_estimate=cost(2 * TOKENS * D * OWN, 2 * TOKENS * D),
        name="preact_share",
    )(acts, w_enc, w_dec)


def codes_kernel(place_ref, got_ref, alive_ref, codes_ref, slope_ref):
    core = place_ref[0]
    codes = []
    for rel in range(2):
        src = core if rel == 0 else 1 - core
        preact = jnp.sum(got_ref[src].astype(f32), axis=0)
        alive = alive_ref[rel].astype(f32)
        codes.append(alive * jax.nn.softplus(preact))
        slope_ref[rel] = alive * jax.nn.sigmoid(preact)
    codes_ref[...] = jnp.concatenate(codes, axis=0).astype(bf16)


def make_codes(place, got, alive):
    held = pl.BlockSpec(memory_space=pltpu.VMEM)
    return pl.pallas_call(
        codes_kernel,
        in_specs=[pl.BlockSpec(memory_space=pltpu.SMEM), held, held],
        out_specs=[held] * 2,
        out_shape=[
            jax.ShapeDtypeStruct((2 * SHARD, OWN), bf16),
            jax.ShapeDtypeStruct((2, SHARD, OWN), f32),
        ],
        compiler_params=params(16),
        cost_estimate=cost(1000000, 2000000),
        name="make_codes",
    )(place, got, alive)


def spread_kernel(*refs):
    out_ref = refs[NX]
    for r in range(NX):
        out_ref[:, r] = jnp.broadcast_to(refs[r][...][None], (LAYERS, 2 * SHARD, OWN))


def spread_codes(parts):
    held = pl.BlockSpec(memory_space=pltpu.VMEM)
    return pl.pallas_call(
        spread_kernel,
        in_specs=[held] * NX,
        out_specs=held,
        out_shape=jax.ShapeDtypeStruct((LAYERS, NX, 2 * SHARD, OWN), bf16),
        compiler_params=params(16),
        cost_estimate=cost(1000000, 2000000),
        name="spread_codes",
    )(*parts)


COLUMNS = 256


def residue_kernel(codes_ref, acts_ref, *rest):
    pieces, rest = rest[:2 * NX], rest[2 * NX:]
    share_ref, keep_ref, send_ref, flat, cols, wide, share, halves, out_sems = rest
    for r in range(NX):
        part = codes_ref[:, r].astype(f32)
        for rel in range(2):
            half = part[:, rel * SHARD:(rel + 1) * SHARD].reshape(HALF, OWN).astype(bf16)
            flat[rel, :, r * OWN:(r + 1) * OWN] = half
            cols[rel, r * OWN:(r + 1) * OWN, :] = pieces[NX * rel + r][...]
    stores = [
        pltpu.make_async_copy(share, share_ref, out_sems.at[0]),
        pltpu.make_async_copy(halves.at[1], send_ref, out_sems.at[1]),
        pltpu.make_async_copy(halves.at[0], keep_ref, out_sems.at[2]),
    ]
    for c in range(WIDE // COLUMNS):
        block = slice(c * COLUMNS, (c + 1) * COLUMNS)
        rebuilt = jnp.dot(flat[0], cols[0, :, block], preferred_element_type=f32)
        rebuilt += jnp.dot(flat[1], cols[1, :, block], preferred_element_type=f32)
        wide[:, block] = (rebuilt * DEC_SCALE - acts_ref[:, block].astype(f32)).astype(bf16)
    for pair in range(NX // 2):
        span = slice(2 * pair * OWN, 2 * (pair + 1) * OWN)
        grads = [
            lax.dot_general(
                wide[...], cols[rel, span, :], (((1,), (1,)), ((), ())), preferred_element_type=f32
            ) * DEC_SCALE
            for rel in range(2)
        ]
        for i in range(2):
            parts = [grads[rel][:, i * OWN:(i + 1) * OWN].reshape(LAYERS, SHARD, OWN) for rel in range(2)]
            share[:, 2 * pair + i] = jnp.concatenate(parts, axis=1).astype(bf16)
    stores[0].start()
    for i, rel in enumerate((1, 0)):
        for c in range(WIDE // COLUMNS):
            block = slice(c * COLUMNS, (c + 1) * COLUMNS)
            grad = lax.dot_general(
                flat[rel], wide[:, block], (((0,), (0,)), ((), ())), preferred_element_type=f32
            ) * DEC_SCALE
            for r in range(NX):
                halves[rel, r, :, block] = grad[r * OWN:(r + 1) * OWN].astype(bf16)
        stores[1 + i].start()
    for copy in stores:
        copy.wait()


def residue_part(codes, acts, pieces):
    held = pl.BlockSpec(memory_space=pltpu.VMEM)
    anywhere = pl.BlockSpec(memory_space=pl.ANY)
    return pl.pallas_call(
        residue_kernel,
        in_specs=[held] * (2 + 2 * NX),
        out_specs=[anywhere] * 3,
        scratch_shapes=[
            pltpu.VMEM((2, HALF, NX * OWN), bf16),
            pltpu.VMEM((2, NX * OWN, WIDE), bf16),
            pltpu.VMEM((HALF, WIDE), bf16),
            pltpu.VMEM((LAYERS, NX, 2 * SHARD, OWN), bf16),
            pltpu.VMEM((2, NX, OWN, WIDE), bf16),
            pltpu.SemaphoreType.DMA((3,)),
        ],
        out_shape=[
            jax.ShapeDtypeStruct((LAYERS, NX, 2 * SHARD, OWN), bf16),
            jax.ShapeDtypeStruct((NX, OWN, WIDE), bf16),
            jax.ShapeDtypeStruct((NX, OWN, WIDE), bf16),
        ],
        compiler_params=params(58),
        cost_estimate=cost(6 * HALF * LAT * WIDE, 10000000),
        name="residue_part",
    )(codes, acts, *pieces)


def join_kernel(keep_ref, got_ref, *outs):
    for r in range(NX):
        outs[r][...] = (keep_ref[r].astype(f32) + got_ref[r].astype(f32)).astype(bf16)


def join_halves(keep, got):
    held = pl.BlockSpec(memory_space=pltpu.VMEM)
    return pl.pallas_call(
        join_kernel,
        in_specs=[held] * 2,
        out_specs=[held] * NX,
        out_shape=[jax.ShapeDtypeStruct((OWN, WIDE), bf16)] * NX,
        compiler_params=params(16),
        cost_estimate=cost(1000000, 4000000),
        name="join_halves",
    )(keep, got)


def decoder_spans(place_ref):
    return [pl.ds(pl.multiple_of(lax.rem(place_ref[1] + r, NX) * WIDE, WIDE), WIDE) for r in range(NX)]


def decoder_fetches(spans, grads, sources, taken, sems):
    fetches = []
    for r, span in enumerate(spans):
        parts = [grads[r]] + [source.at[:, span] for source in sources]
        fetches.append([pltpu.make_async_copy(part, taken.at[r, i], sems.at[r, i]) for i, part in enumerate(parts)])
    for copies in fetches:
        for copy in copies:
            copy.start()
    return fetches


def decoder_step(fetches, taken, r):
    for copy in fetches[r]:
        copy.wait()
    grad, w, m, v = (taken[r, i].astype(f32) for i in range(4))
    return adam_step(w, grad, m, v)


def size_kernel(place_ref, *refs):
    grads, (w_ref, m_ref, v_ref, rms_out) = refs[:NX], refs[NX:]
    total = jnp.zeros((OWN, OWN), f32)
    for r, span in enumerate(decoder_spans(place_ref)):
        grad, w, m, v = (part.astype(f32) for part in (grads[r][...], w_ref[:, span], m_ref[:, span], v_ref[:, span]))
        stepped = adam_step(w, grad, m, v)[0]
        square = stepped * stepped
        for c in range(WIDE // OWN):
            total += square[:, c * OWN:(c + 1) * OWN]
    rms = jnp.sqrt(jnp.sum(total.T, axis=0, keepdims=True) * (1.0 / D) + 1e-06)
    rms_out[...] = jnp.broadcast_to(rms, (8, OWN))


def decoder_size(place, grads, w, m, v):
    held = pl.BlockSpec(memory_space=pltpu.VMEM)
    return pl.pallas_call(
        size_kernel,
        in_specs=[pl.BlockSpec(memory_space=pltpu.SMEM)] + [held] * (NX + 3),
        out_specs=held,
        out_shape=jax.ShapeDtypeStruct((8, OWN), f32),
        compiler_params=params(24),
        cost_estimate=cost(20 * OWN * D, 4000000),
        name="decoder_size",
    )(place, *grads, w, m, v)


def decoder_kernel(place_ref, *refs):
    grads, (w_ref, m_ref, v_ref, *rest) = refs[:NX], refs[NX:]
    m_out, v_out, stepped_out, taken, moved, held, in_sems, out_sems = rest
    spans = decoder_spans(place_ref)
    fetches = decoder_fetches(spans, grads, (w_ref, m_ref, v_ref), taken, in_sems)
    stores = []
    for r in range(NX):
        stepped, one, two = decoder_step(fetches, taken, r)
        moved[r, 0] = one.astype(bf16)
        moved[r, 1] = two.astype(bf16)
        held[r] = stepped
        sources = (moved.at[r, 0], moved.at[r, 1], held.at[r])
        for i, target in enumerate((m_out, v_out, stepped_out)):
            stores.append(pltpu.make_async_copy(sources[i], target.at[:, spans[r]], out_sems.at[r, i]))
            stores[-1].start()
    for copy in stores:
        copy.wait()


def decoder_adam(place, grads, w, m, v):
    anywhere = pl.BlockSpec(memory_space=pl.ANY)
    return pl.pallas_call(
        decoder_kernel,
        in_specs=[pl.BlockSpec(memory_space=pltpu.SMEM)] + [anywhere] * (NX + 3),
        out_specs=[anywhere] * 3,
        out_shape=[
            jax.ShapeDtypeStruct((OWN, D), bf16),
            jax.ShapeDtypeStruct((OWN, D), bf16),
            jax.ShapeDtypeStruct((OWN, D), f32),
        ],
        scratch_shapes=[
            pltpu.VMEM((NX, 4, OWN, WIDE), bf16),
            pltpu.VMEM((NX, 2, OWN, WIDE), bf16),
            pltpu.VMEM((NX, OWN, WIDE), f32),
            pltpu.SemaphoreType.DMA((NX, 4)),
            pltpu.SemaphoreType.DMA((NX, 3)),
        ],
        compiler_params=params(54),
        cost_estimate=cost(20 * OWN * D, 8000000),
        name="decoder_adam",
    )(place, *grads, w, m, v)


def sum_kernel(got_ref, keep_ref, *outs):
    for r in range(NX):
        both = jnp.sum(got_ref[:, r].astype(f32), axis=0)
        for rel in range(2):
            total = both[rel * SHARD:(rel + 1) * SHARD]
            if r == 0:
                keep_ref[rel] = total
            else:
                outs[r - 1][rel] = total.astype(bf16)


def sum_layers(got):
    return pl.pallas_call(
        sum_kernel,
        in_specs=[pl.BlockSpec(memory_space=pltpu.VMEM)],
        out_specs=[pl.BlockSpec(memory_space=pltpu.VMEM)] * NX,
        out_shape=[jax.ShapeDtypeStruct((2, SHARD, OWN), f32)]
        + [jax.ShapeDtypeStruct((2, SHARD, OWN), bf16)] * (NX - 1),
        compiler_params=params(16),
        cost_estimate=cost(1000000, 2000000),
        name="sum_layers",
    )(got)


def grad_pre_kernel(core_ref, keep_ref, one_ref, two_ref, three_ref, slope_ref, rms_ref, out_ref):
    core = core_ref[0]
    rms = rms_ref[...]
    high = rms.astype(bf16).astype(f32)
    mid = (rms - high).astype(bf16).astype(f32)
    low = rms - high - mid
    row = lax.broadcasted_iota(jnp.int32, (8, OWN), 0)
    tail = jnp.where(row == 0, high, jnp.where(row == 1, mid, jnp.where(row == 2, low, 0.0)))
    for rel in range(2):
        grad = keep_ref[rel] + one_ref[rel].astype(f32) + two_ref[rel].astype(f32) + three_ref[rel].astype(f32)
        message = jnp.concatenate([grad * slope_ref[rel], tail], axis=0).astype(bf16)
        dest = core if rel == 0 else 1 - core
        out_ref[dest] = jnp.broadcast_to(message[None], (LAYERS, MESSAGE, OWN))


def make_grad_pre(core, parts, slope, rms):
    return pl.pallas_call(
        grad_pre_kernel,
        in_specs=[pl.BlockSpec(memory_space=pltpu.SMEM)] + [pl.BlockSpec(memory_space=pltpu.VMEM)] * 6,
        out_specs=pl.BlockSpec(memory_space=pltpu.VMEM),
        out_shape=jax.ShapeDtypeStruct((2, LAYERS, MESSAGE, OWN), bf16),
        compiler_params=params(16),
        cost_estimate=cost(1000000, 2000000),
        name="make_grad_pre",
    )(core, *parts, slope, rms)


PART = 1024
PARTS = D // PART


def encoder_kernel(core_ref, got_ref, w_ref, m_ref, v_ref, acts_ref, dec_ref, *rest):
    w_out, m_out, v_out, dec_out, acts, dec, w_new, m_new, v_new, dec_new, turned, in_sems, out_sems = rest

    def span(c):
        return pl.ds(pl.multiple_of(c * PART, PART), PART)

    def fetches(c):
        return (
            pltpu.make_async_copy(acts_ref.at[:, span(c)], acts.at[c], in_sems.at[c, 0]),
            pltpu.make_async_copy(dec_ref.at[:, span(c)], dec.at[c], in_sems.at[c, 1]),
        )

    def stores(c):
        return (
            pltpu.make_async_copy(w_new.at[c], w_out.at[span(c)], out_sems.at[c, 0]),
            pltpu.make_async_copy(m_new.at[c], m_out.at[span(c)], out_sems.at[c, 1]),
            pltpu.make_async_copy(v_new.at[c], v_out.at[span(c)], out_sems.at[c, 2]),
            pltpu.make_async_copy(dec_new.at[c], dec_out.at[:, span(c)], out_sems.at[c, 3]),
        )

    @pl.loop(0, PARTS)
    def _(c):
        for copy in fetches(c):
            copy.start()

    got = got_ref[...].astype(f32)
    turned[...] = got[:, :, :SHARD].reshape(TOKENS, OWN).T.astype(bf16)
    rms = jnp.sum(got_ref[core_ref[0]].astype(f32)[:, SHARD:], axis=0)
    row = jnp.sum(rms[:3], axis=0, keepdims=True) * (1.0 / LAYERS)
    column = jnp.broadcast_to(row, (OWN, OWN)).T[:, :1]

    @pl.loop(0, PARTS)
    def _(c):
        for copy in fetches(c):
            copy.wait()
        grad = jnp.dot(turned[...], acts[c], preferred_element_type=f32) * ENC_SCALE
        grad = grad.astype(bf16).astype(f32).T
        stepped, one, two = adam_step(
            w_ref[span(c), :].astype(f32), grad, m_ref[span(c), :].astype(f32), v_ref[span(c), :].astype(f32)
        )
        w_new[c] = (stepped * row).astype(bf16)
        m_new[c] = one.astype(bf16)
        v_new[c] = two.astype(bf16)
        dec_new[c] = (dec[c] / column).astype(bf16)
        for copy in stores(c):
            copy.start()

    @pl.loop(0, PARTS)
    def _(c):
        for copy in stores(c):
            copy.wait()


def encoder_adam(core, got, acts, w, m, v, stepped_dec):
    held = pl.BlockSpec(memory_space=pltpu.VMEM)
    anywhere = pl.BlockSpec(memory_space=pl.ANY)
    return pl.pallas_call(
        encoder_kernel,
        in_specs=[pl.BlockSpec(memory_space=pltpu.SMEM)] + [held] * 4 + [anywhere] * 2,
        out_specs=[anywhere] * 4,
        out_shape=[jax.ShapeDtypeStruct((D, OWN), bf16)] * 3 + [jax.ShapeDtypeStruct((OWN, D), bf16)],
        scratch_shapes=[
            pltpu.VMEM((PARTS, TOKENS, PART), bf16),
            pltpu.VMEM((PARTS, OWN, PART), f32),
            pltpu.VMEM((PARTS, PART, OWN), bf16),
            pltpu.VMEM((PARTS, PART, OWN), bf16),
            pltpu.VMEM((PARTS, PART, OWN), bf16),
            pltpu.VMEM((PARTS, OWN, PART), bf16),
            pltpu.VMEM((OWN, TOKENS), bf16),
            pltpu.SemaphoreType.DMA((PARTS, 2)),
            pltpu.SemaphoreType.DMA((PARTS, 4)),
        ],
        compiler_params=params(52),
        cost_estimate=cost(2 * TOKENS * D * OWN, 20000000),
        name="encoder_adam",
    )(core, got, w, m, v, acts, stepped_dec)


def swap(array):
    return lax.ppermute(array, "core", [(0, 1), (1, 0)])


def shift(array, steps):
    return lax.ppermute(array, "x", [(i, (i + steps) % NX) for i in range(NX)])


def exchange(array, axes):
    flat = array.reshape(-1, array.shape[-1])
    return lax.all_to_all(flat, axes, split_axis=0, concat_axis=0, tiled=True).reshape(array.shape)


LAYER_AXES = ("y", "z")
TOKEN_AXES = ("core", "y", "z")


def local(acts, active, w_enc, m_enc, v_enc, w_dec, m_dec, v_dec):
    core = lax.axis_index("core")
    layer = lax.axis_index(LAYER_AXES)
    place = jnp.stack([core, lax.axis_index("x")]).astype(jnp.int32)
    acts, w_dec, m_dec, v_dec = (array[:, 0, :] for array in (acts, w_dec, m_dec, v_dec))

    alive = active.astype(bf16).reshape(2, LAYERS, SHARD, OWN)
    alive = lax.dynamic_index_in_dim(alive, layer, 1, keepdims=False)
    alive_own = lax.dynamic_index_in_dim(alive, core, 0, keepdims=False)
    alive_other = swap(lax.dynamic_index_in_dim(alive, 1 - core, 0, keepdims=False))
    alive = jnp.stack([alive_own, alive_other])

    share, *mine = preact_share(acts, w_enc[0], w_dec)
    own_cols = [mine[0]] + [shift(mine[r], r) for r in range(1, NX)]
    share = exchange(share.reshape(2, LAYERS, SHARD, OWN), TOKEN_AXES)
    codes, slope = make_codes(place, share, alive)
    codes = spread_codes([codes] + [shift(codes, r) for r in range(1, NX)])
    codes = exchange(codes, LAYER_AXES)
    other_cols = [swap(piece) for piece in own_cols]
    own_acts = lax.dynamic_slice(acts, (core * HALF, lax.axis_index("x") * WIDE), (HALF, WIDE))
    grad_share, keep, send = residue_part(codes, own_acts, own_cols + other_cols)
    grad_share = exchange(grad_share, LAYER_AXES)

    grad_dec = join_halves(keep, swap(send))
    grad_dec = [grad_dec[0]] + [shift(grad_dec[r], NX - r) for r in range(1, NX)]
    rms = decoder_size(place, grad_dec, w_dec, m_dec, v_dec)
    m_dec_new, v_dec_new, stepped_dec = decoder_adam(place, grad_dec, w_dec, m_dec, v_dec)

    parts = sum_layers(grad_share)
    parts = [parts[0]] + [shift(parts[r], NX - r) for r in range(1, NX)]
    messages = exchange(make_grad_pre(place, parts, slope, rms), TOKEN_AXES)
    w_enc_new, m_enc_new, v_enc_new, w_dec_new = encoder_adam(
        place, messages, acts, w_enc[0], m_enc[0], v_enc[0], stepped_dec
    )
    return (
        w_enc_new[None],
        m_enc_new[None],
        v_enc_new[None],
        w_dec_new[:, None, :],
        m_dec_new[:, None, :],
        v_dec_new[:, None, :],
    )


def solution(mesh):
    fine = Mesh(mesh.devices.reshape(4, 4, NX, 2), ("y", "z", "x", "core"))
    layer = ("y", "z")
    latent = ("x", "core")
    return jax.shard_map(
        local,
        mesh=fine,
        in_specs=(
            P(None, layer, None),
            P(None, latent),
            P(layer, None, latent),
            P(layer, None, latent),
            P(layer, None, latent),
            P(latent, layer, None),
            P(latent, layer, None),
            P(latent, layer, None),
        ),
        out_specs=(
            P(layer, None, latent),
            P(layer, None, latent),
            P(layer, None, latent),
            P(latent, layer, None),
            P(latent, layer, None),
            P(latent, layer, None),
        ),
        check_vma=False,
    )
```

```python
import jax
import jax.numpy as jnp
from jax import lax
from jax.experimental import pallas as pl
from jax.experimental.pallas import tpu as pltpu
from jax.sharding import Mesh
from jax.sharding import PartitionSpec as P

D = 4096
LAT = 1024
TOKENS = 1280
LAYERS = 16
NX = 4
HALF = TOKENS // 2
SHARD = HALF // LAYERS
OWN = 128
WIDE = D // NX
ENC_SCALE = (LAYERS * D) ** (-0.5)
DEC_SCALE = LAT ** (-0.5)
MESSAGE = 96

bf16 = jnp.bfloat16
f32 = jnp.float32


def params(mib=48):
    return pltpu.CompilerParams(vmem_limit_bytes=mib * 1024 * 1024)


def cost(flops, nbytes):
    return pl.CostEstimate(flops=flops, bytes_accessed=nbytes, transcendentals=0)


def adam_step(weights, gradient, moment_one, moment_two):
    one_new = 0.9 * moment_one + 0.1 * gradient
    two_new = 0.999 * moment_two + 0.001 * gradient * gradient
    stepped = weights - 0.05 * one_new / (jnp.sqrt(two_new) + 1e-08)
    return (stepped, one_new, two_new)


CHUNKS = 8
CHUNK = TOKENS // CHUNKS
BLOCKS = CHUNK // SHARD


def preact_kernel(acts_ref, w_ref, dec_ref, out_ref, *rest):
    pieces, (own_ref, rows, weights, dec, row_sems, weight_sem, cut_sems, own_sems) = rest[:NX], rest[NX:]
    here, core = lax.axis_index("x"), lax.axis_index("core")
    width = pl.ds(pl.multiple_of(here * WIDE, WIDE), WIDE)
    fetch = pltpu.make_async_copy(w_ref, weights, weight_sem)
    fetch.start()

    def block(c):
        source = acts_ref.at[pl.ds(pl.multiple_of(c * CHUNK, CHUNK), CHUNK)]
        return pltpu.make_async_copy(source, rows.at[c], row_sems.at[c])

    block(0).start()
    block(1).start()
    cuts = []
    for r in range(NX):
        start = pl.multiple_of(lax.rem(here + r, NX) * WIDE, WIDE)
        cuts.append((
            pltpu.make_async_copy(dec_ref.at[:, pl.ds(start, WIDE)], dec.at[r], cut_sems.at[0, r]),
            pltpu.make_async_copy(dec.at[r], pieces[r], cut_sems.at[1, r]),
        ))
        cuts[r][0].start()

    @pl.loop(2, CHUNKS)
    def _(c):
        block(c).start()

    def own(c):
        place = lax.rem(c, CHUNKS // 2)
        target = own_ref.at[pl.ds(pl.multiple_of(place * CHUNK, CHUNK), CHUNK)]
        return pltpu.make_async_copy(rows.at[c, :, width], target, own_sems.at[place])

    def multiply(c, half):
        block(c).wait()

        @pl.when(core == half)
        def _():
            own(c).start()

        share = jnp.dot(rows[c], weights[...], preferred_element_type=f32)
        blocks = pl.ds((c - half * (CHUNKS // 2)) * BLOCKS, BLOCKS)
        out_ref[blocks, half] = (share * ENC_SCALE).reshape(BLOCKS, SHARD, OWN).astype(bf16)

    fetch.wait()

    @pl.loop(0, CHUNKS // 2)
    def _(c):
        multiply(c, 0)

    for take, give in cuts:
        take.wait()
        give.start()

    @pl.loop(CHUNKS // 2, CHUNKS)
    def _(c):
        multiply(c, 1)

    for _, give in cuts:
        give.wait()

    @pl.loop(0, CHUNKS // 2)
    def _(c):
        own(c + core * (CHUNKS // 2)).wait()


def preact_share(acts, w_enc, w_dec):
    anywhere = pl.BlockSpec(memory_space=pl.ANY)
    return pl.pallas_call(
        preact_kernel,
        in_specs=[anywhere] * 3,
        out_specs=[pl.BlockSpec(memory_space=pltpu.VMEM)] + [anywhere] * (NX + 1),
        out_shape=[jax.ShapeDtypeStruct((LAYERS, 2, SHARD, OWN), bf16)]
        + [jax.ShapeDtypeStruct((OWN, WIDE), bf16)] * NX
        + [jax.ShapeDtypeStruct((HALF, WIDE), bf16)],
        scratch_shapes=[
            pltpu.VMEM((CHUNKS, CHUNK, D), bf16),
            pltpu.VMEM((D, OWN), bf16),
            pltpu.VMEM((NX, OWN, WIDE), bf16),
            pltpu.SemaphoreType.DMA((CHUNKS,)),
            pltpu.SemaphoreType.DMA,
            pltpu.SemaphoreType.DMA((2, NX)),
            pltpu.SemaphoreType.DMA((CHUNKS // 2,)),
        ],
        compiler_params=params(60),
        cost_estimate=cost(2 * TOKENS * D * OWN, 2 * TOKENS * D),
        name="preact_share",
    )(acts, w_enc, w_dec)


def codes_kernel(got_ref, alive_ref, codes_ref, slope_ref):
    preact = jnp.sum(got_ref[...].astype(f32), axis=0)
    alive = alive_ref[...].astype(f32)
    codes_ref[...] = (alive * jax.nn.softplus(preact)).astype(bf16)
    slope_ref[...] = alive * jax.nn.sigmoid(preact)


def make_codes(got, alive):
    held = pl.BlockSpec(memory_space=pltpu.VMEM)
    return pl.pallas_call(
        codes_kernel,
        in_specs=[held] * 2,
        out_specs=[held] * 2,
        out_shape=[
            jax.ShapeDtypeStruct((2, SHARD, OWN), bf16),
            jax.ShapeDtypeStruct((2, SHARD, OWN), f32),
        ],
        compiler_params=params(16),
        cost_estimate=cost(1000000, 2000000),
        name="make_codes",
    )(got, alive)


def spread_kernel(*refs):
    out_ref = refs[NX]
    for r in range(NX):
        for half in range(2):
            out_ref[half, :, r] = jnp.broadcast_to(refs[r][half][None], (LAYERS, SHARD, OWN))


def spread_codes(parts):
    held = pl.BlockSpec(memory_space=pltpu.VMEM)
    return pl.pallas_call(
        spread_kernel,
        in_specs=[held] * NX,
        out_specs=held,
        out_shape=jax.ShapeDtypeStruct((2, LAYERS, NX, SHARD, OWN), bf16),
        compiler_params=params(16),
        cost_estimate=cost(1000000, 2000000),
        name="spread_codes",
    )(*parts)


COLUMNS = 256


def residue_kernel(codes_ref, acts_ref, *rest):
    core = lax.axis_index("core")
    order = (core, 1 - core)
    pieces, rest = rest[:2 * NX], rest[2 * NX:]
    share_ref, keep_ref, send_ref, flat, cols, wide, share, halves, out_sems = rest
    for r in range(NX):
        for rel in range(2):
            part = codes_ref[order[rel], :, r].astype(f32)
            flat[rel, :, r * OWN:(r + 1) * OWN] = part.reshape(HALF, OWN).astype(bf16)
            cols[rel, r * OWN:(r + 1) * OWN, :] = pieces[NX * rel + r][...]
    stores = [
        pltpu.make_async_copy(share, share_ref, out_sems.at[0]),
        pltpu.make_async_copy(halves.at[1], send_ref, out_sems.at[1]),
        pltpu.make_async_copy(halves.at[0], keep_ref, out_sems.at[2]),
    ]
    for c in range(WIDE // COLUMNS):
        block = slice(c * COLUMNS, (c + 1) * COLUMNS)
        rebuilt = jnp.dot(flat[0], cols[0, :, block], preferred_element_type=f32)
        rebuilt += jnp.dot(flat[1], cols[1, :, block], preferred_element_type=f32)
        wide[:, block] = (rebuilt * DEC_SCALE - acts_ref[:, block].astype(f32)).astype(bf16)
    for pair in range(NX // 2):
        span = slice(2 * pair * OWN, 2 * (pair + 1) * OWN)
        grads = [
            lax.dot_general(
                wide[...], cols[rel, span, :], (((1,), (1,)), ((), ())), preferred_element_type=f32
            ) * DEC_SCALE
            for rel in range(2)
        ]
        for i in range(2):
            for rel in range(2):
                part = grads[rel][:, i * OWN:(i + 1) * OWN].reshape(LAYERS, SHARD, OWN)
                share[order[rel], :, 2 * pair + i] = part.astype(bf16)
    stores[0].start()
    for i, rel in enumerate((1, 0)):
        for c in range(WIDE // COLUMNS):
            block = slice(c * COLUMNS, (c + 1) * COLUMNS)
            grad = lax.dot_general(
                flat[rel], wide[:, block], (((0,), (0,)), ((), ())), preferred_element_type=f32
            ) * DEC_SCALE
            for r in range(NX):
                halves[rel, r, :, block] = grad[r * OWN:(r + 1) * OWN].astype(bf16)
        stores[1 + i].start()
    for copy in stores:
        copy.wait()


def residue_part(codes, acts, pieces):
    held = pl.BlockSpec(memory_space=pltpu.VMEM)
    anywhere = pl.BlockSpec(memory_space=pl.ANY)
    return pl.pallas_call(
        residue_kernel,
        in_specs=[held] * (2 + 2 * NX),
        out_specs=[anywhere] * 3,
        scratch_shapes=[
            pltpu.VMEM((2, HALF, NX * OWN), bf16),
            pltpu.VMEM((2, NX * OWN, WIDE), bf16),
            pltpu.VMEM((HALF, WIDE), bf16),
            pltpu.VMEM((2, LAYERS, NX, SHARD, OWN), bf16),
            pltpu.VMEM((2, NX, OWN, WIDE), bf16),
            pltpu.SemaphoreType.DMA((3,)),
        ],
        out_shape=[
            jax.ShapeDtypeStruct((2, LAYERS, NX, SHARD, OWN), bf16),
            jax.ShapeDtypeStruct((NX, OWN, WIDE), bf16),
            jax.ShapeDtypeStruct((NX, OWN, WIDE), bf16),
        ],
        compiler_params=params(58),
        cost_estimate=cost(6 * HALF * LAT * WIDE, 10000000),
        name="residue_part",
    )(codes, acts, *pieces)


def join_kernel(keep_ref, got_ref, *outs):
    for r in range(NX):
        outs[r][...] = (keep_ref[r].astype(f32) + got_ref[r].astype(f32)).astype(bf16)


def join_halves(keep, got):
    held = pl.BlockSpec(memory_space=pltpu.VMEM)
    return pl.pallas_call(
        join_kernel,
        in_specs=[held] * 2,
        out_specs=[held] * NX,
        out_shape=[jax.ShapeDtypeStruct((OWN, WIDE), bf16)] * NX,
        compiler_params=params(16),
        cost_estimate=cost(1000000, 4000000),
        name="join_halves",
    )(keep, got)


def decoder_spans(place_ref):
    return [pl.ds(pl.multiple_of(lax.rem(place_ref[1] + r, NX) * WIDE, WIDE), WIDE) for r in range(NX)]


def decoder_fetches(spans, grads, sources, taken, sems):
    fetches = []
    for r, span in enumerate(spans):
        parts = [grads[r]] + [source.at[:, span] for source in sources]
        fetches.append([pltpu.make_async_copy(part, taken.at[r, i], sems.at[r, i]) for i, part in enumerate(parts)])
    for copies in fetches:
        for copy in copies:
            copy.start()
    return fetches


def decoder_step(fetches, taken, r):
    for copy in fetches[r]:
        copy.wait()
    grad, w, m, v = (taken[r, i].astype(f32) for i in range(4))
    return adam_step(w, grad, m, v)


def size_kernel(place_ref, *refs):
    grads, (w_ref, m_ref, v_ref, rms_out) = refs[:NX], refs[NX:]
    total = jnp.zeros((OWN, OWN), f32)
    for r, span in enumerate(decoder_spans(place_ref)):
        grad, w, m, v = (part.astype(f32) for part in (grads[r][...], w_ref[:, span], m_ref[:, span], v_ref[:, span]))
        stepped = adam_step(w, grad, m, v)[0]
        square = stepped * stepped
        for c in range(WIDE // OWN):
            total += square[:, c * OWN:(c + 1) * OWN]
    rms = jnp.sqrt(jnp.sum(total.T, axis=0, keepdims=True) * (1.0 / D) + 1e-06)
    rms_out[...] = jnp.broadcast_to(rms, (8, OWN))


def decoder_size(place, grads, w, m, v):
    held = pl.BlockSpec(memory_space=pltpu.VMEM)
    return pl.pallas_call(
        size_kernel,
        in_specs=[pl.BlockSpec(memory_space=pltpu.SMEM)] + [held] * (NX + 3),
        out_specs=held,
        out_shape=jax.ShapeDtypeStruct((8, OWN), f32),
        compiler_params=params(24),
        cost_estimate=cost(20 * OWN * D, 4000000),
        name="decoder_size",
    )(place, *grads, w, m, v)


def decoder_kernel(place_ref, *refs):
    grads, (w_ref, m_ref, v_ref, *rest) = refs[:NX], refs[NX:]
    m_out, v_out, stepped_out, taken, moved, held, in_sems, out_sems = rest
    spans = decoder_spans(place_ref)
    fetches = decoder_fetches(spans, grads, (w_ref, m_ref, v_ref), taken, in_sems)
    stores = []
    for r in range(NX):
        stepped, one, two = decoder_step(fetches, taken, r)
        moved[r, 0] = one.astype(bf16)
        moved[r, 1] = two.astype(bf16)
        held[r] = stepped
        sources = (moved.at[r, 0], moved.at[r, 1], held.at[r])
        for i, target in enumerate((m_out, v_out, stepped_out)):
            stores.append(pltpu.make_async_copy(sources[i], target.at[:, spans[r]], out_sems.at[r, i]))
            stores[-1].start()
    for copy in stores:
        copy.wait()


def decoder_adam(place, grads, w, m, v):
    anywhere = pl.BlockSpec(memory_space=pl.ANY)
    return pl.pallas_call(
        decoder_kernel,
        in_specs=[pl.BlockSpec(memory_space=pltpu.SMEM)] + [anywhere] * (NX + 3),
        out_specs=[anywhere] * 3,
        out_shape=[
            jax.ShapeDtypeStruct((OWN, D), bf16),
            jax.ShapeDtypeStruct((OWN, D), bf16),
            jax.ShapeDtypeStruct((OWN, D), f32),
        ],
        scratch_shapes=[
            pltpu.VMEM((NX, 4, OWN, WIDE), bf16),
            pltpu.VMEM((NX, 2, OWN, WIDE), bf16),
            pltpu.VMEM((NX, OWN, WIDE), f32),
            pltpu.SemaphoreType.DMA((NX, 4)),
            pltpu.SemaphoreType.DMA((NX, 3)),
        ],
        compiler_params=params(54),
        cost_estimate=cost(20 * OWN * D, 8000000),
        name="decoder_adam",
    )(place, *grads, w, m, v)


def sum_kernel(got_ref, keep_ref, *outs):
    for r in range(NX):
        total = jnp.sum(got_ref[:, :, r].astype(f32), axis=1)
        if r == 0:
            keep_ref[...] = total
        else:
            outs[r - 1][...] = total.astype(bf16)


def sum_layers(got):
    held = pl.BlockSpec(memory_space=pltpu.VMEM)
    return pl.pallas_call(
        sum_kernel,
        in_specs=[held],
        out_specs=[held] * NX,
        out_shape=[jax.ShapeDtypeStruct((2, SHARD, OWN), f32)]
        + [jax.ShapeDtypeStruct((2, SHARD, OWN), bf16)] * (NX - 1),
        compiler_params=params(16),
        cost_estimate=cost(1000000, 2000000),
        name="sum_layers",
    )(got)


def grad_pre_kernel(zero_ref, one_ref, two_ref, three_ref, slope_ref, rms_ref, out_ref):
    rms = rms_ref[...]
    high = rms.astype(bf16).astype(f32)
    mid = (rms - high).astype(bf16).astype(f32)
    low = rms - high - mid
    row = lax.broadcasted_iota(jnp.int32, (8, OWN), 0)
    tail = jnp.where(row == 0, high, jnp.where(row == 1, mid, jnp.where(row == 2, low, 0.0)))
    grad = sum(ref[...].astype(f32) for ref in (zero_ref, one_ref, two_ref, three_ref)) * slope_ref[...]
    message = jnp.concatenate([grad.reshape(2 * SHARD, OWN), tail, jnp.zeros((8, OWN), f32)], axis=0)
    out_ref[...] = jnp.broadcast_to(message.astype(bf16)[None], (LAYERS, MESSAGE, OWN))


def make_grad_pre(parts, slope, rms):
    held = pl.BlockSpec(memory_space=pltpu.VMEM)
    return pl.pallas_call(
        grad_pre_kernel,
        in_specs=[held] * 6,
        out_specs=held,
        out_shape=jax.ShapeDtypeStruct((LAYERS, MESSAGE, OWN), bf16),
        compiler_params=params(16),
        cost_estimate=cost(1000000, 2000000),
        name="make_grad_pre",
    )(*parts, slope, rms)


PART = 1024
PARTS = D // PART


def encoder_kernel(got_ref, w_ref, m_ref, v_ref, acts_ref, dec_ref, *rest):
    w_out, m_out, v_out, dec_out, acts, dec, w_new, m_new, v_new, dec_new, turned, in_sems, out_sems = rest

    def span(c):
        return pl.ds(pl.multiple_of(c * PART, PART), PART)

    def fetches(c):
        return (
            pltpu.make_async_copy(acts_ref.at[:, span(c)], acts.at[c], in_sems.at[c, 0]),
            pltpu.make_async_copy(dec_ref.at[:, span(c)], dec.at[c], in_sems.at[c, 1]),
        )

    def stores(c):
        return (
            pltpu.make_async_copy(w_new.at[c], w_out.at[span(c)], out_sems.at[c, 0]),
            pltpu.make_async_copy(m_new.at[c], m_out.at[span(c)], out_sems.at[c, 1]),
            pltpu.make_async_copy(v_new.at[c], v_out.at[span(c)], out_sems.at[c, 2]),
            pltpu.make_async_copy(dec_new.at[c], dec_out.at[:, span(c)], out_sems.at[c, 3]),
        )

    @pl.loop(0, PARTS)
    def _(c):
        for copy in fetches(c):
            copy.start()

    got = got_ref[...].astype(f32)
    for half in range(2):
        grad_pre = got[:, half * SHARD:(half + 1) * SHARD].reshape(HALF, OWN)
        turned[:, half * HALF:(half + 1) * HALF] = grad_pre.T.astype(bf16)
    rms = jnp.sum(got[:, 2 * SHARD:], axis=0)
    row = jnp.sum(rms[:3], axis=0, keepdims=True) * (1.0 / LAYERS)
    column = jnp.broadcast_to(row, (OWN, OWN)).T[:, :1]

    @pl.loop(0, PARTS)
    def _(c):
        for copy in fetches(c):
            copy.wait()
        grad = jnp.dot(turned[...], acts[c], preferred_element_type=f32) * ENC_SCALE
        grad = grad.astype(bf16).astype(f32).T
        stepped, one, two = adam_step(
            w_ref[span(c), :].astype(f32), grad, m_ref[span(c), :].astype(f32), v_ref[span(c), :].astype(f32)
        )
        w_new[c] = (stepped * row).astype(bf16)
        m_new[c] = one.astype(bf16)
        v_new[c] = two.astype(bf16)
        dec_new[c] = (dec[c] / column).astype(bf16)
        for copy in stores(c):
            copy.start()

    @pl.loop(0, PARTS)
    def _(c):
        for copy in stores(c):
            copy.wait()


def encoder_adam(got, acts, w, m, v, stepped_dec):
    held = pl.BlockSpec(memory_space=pltpu.VMEM)
    anywhere = pl.BlockSpec(memory_space=pl.ANY)
    return pl.pallas_call(
        encoder_kernel,
        in_specs=[held] * 4 + [anywhere] * 2,
        out_specs=[anywhere] * 4,
        out_shape=[jax.ShapeDtypeStruct((D, OWN), bf16)] * 3 + [jax.ShapeDtypeStruct((OWN, D), bf16)],
        scratch_shapes=[
            pltpu.VMEM((PARTS, TOKENS, PART), bf16),
            pltpu.VMEM((PARTS, OWN, PART), f32),
            pltpu.VMEM((PARTS, PART, OWN), bf16),
            pltpu.VMEM((PARTS, PART, OWN), bf16),
            pltpu.VMEM((PARTS, PART, OWN), bf16),
            pltpu.VMEM((PARTS, OWN, PART), bf16),
            pltpu.VMEM((OWN, TOKENS), bf16),
            pltpu.SemaphoreType.DMA((PARTS, 2)),
            pltpu.SemaphoreType.DMA((PARTS, 4)),
        ],
        compiler_params=params(52),
        cost_estimate=cost(2 * TOKENS * D * OWN, 20000000),
        name="encoder_adam",
    )(got, w, m, v, acts, stepped_dec)


def swap(array):
    return lax.ppermute(array, "core", [(0, 1), (1, 0)])


def shift(array, steps):
    return lax.ppermute(array, "x", [(i, (i + steps) % NX) for i in range(NX)])


def exchange(array, axes):
    flat = array.reshape(-1, array.shape[-1])
    return lax.all_to_all(flat, axes, split_axis=0, concat_axis=0, tiled=True).reshape(array.shape)


LAYER_AXES = ("y", "z")
TOKEN_AXES = ("core", "y", "z")


def local(acts, active, w_enc, m_enc, v_enc, w_dec, m_dec, v_dec):
    core = lax.axis_index("core")
    layer = lax.axis_index(LAYER_AXES)
    place = jnp.stack([core, lax.axis_index("x")]).astype(jnp.int32)
    acts, w_dec, m_dec, v_dec = (array[:, 0, :] for array in (acts, w_dec, m_dec, v_dec))

    alive = active.astype(bf16).reshape(2, LAYERS, SHARD, OWN)
    alive = lax.dynamic_index_in_dim(alive, layer, 1, keepdims=False)

    share, *mine, own_acts = preact_share(acts, w_enc[0], w_dec)
    own_cols = [mine[0]] + [shift(mine[r], r) for r in range(1, NX)]
    codes, slope = make_codes(exchange(share, LAYER_AXES), alive)
    codes = spread_codes([codes] + [shift(codes, r) for r in range(1, NX)])
    codes = exchange(codes, TOKEN_AXES)
    other_cols = [swap(piece) for piece in own_cols]
    grad_share, keep, send = residue_part(codes, own_acts, own_cols + other_cols)
    grad_share = exchange(grad_share, TOKEN_AXES)

    grad_dec = join_halves(keep, swap(send))
    grad_dec = [grad_dec[0]] + [shift(grad_dec[r], NX - r) for r in range(1, NX)]
    rms = decoder_size(place, grad_dec, w_dec, m_dec, v_dec)
    m_dec_new, v_dec_new, stepped_dec = decoder_adam(place, grad_dec, w_dec, m_dec, v_dec)

    parts = sum_layers(grad_share)
    parts = [parts[0]] + [shift(parts[r], NX - r) for r in range(1, NX)]
    messages = exchange(make_grad_pre(parts, slope, rms), LAYER_AXES)
    w_enc_new, m_enc_new, v_enc_new, w_dec_new = encoder_adam(
        messages, acts, w_enc[0], m_enc[0], v_enc[0], stepped_dec
    )
    return (
        w_enc_new[None],
        m_enc_new[None],
        v_enc_new[None],
        w_dec_new[:, None, :],
        m_dec_new[:, None, :],
        v_dec_new[:, None, :],
    )


def solution(mesh):
    fine = Mesh(mesh.devices.reshape(4, 4, NX, 2), ("y", "z", "x", "core"))
    layer = ("y", "z")
    latent = ("x", "core")
    return jax.shard_map(
        local,
        mesh=fine,
        in_specs=(
            P(None, layer, None),
            P(None, latent),
            P(layer, None, latent),
            P(layer, None, latent),
            P(layer, None, latent),
            P(latent, layer, None),
            P(latent, layer, None),
            P(latent, layer, None),
        ),
        out_specs=(
            P(layer, None, latent),
            P(layer, None, latent),
            P(layer, None, latent),
            P(latent, layer, None),
            P(latent, layer, None),
            P(latent, layer, None),
        ),
        check_vma=False,
    )
```

```python
import jax
import jax.numpy as jnp
from jax import lax
from jax.experimental import pallas as pl
from jax.experimental.pallas import tpu as pltpu
from jax.sharding import Mesh
from jax.sharding import PartitionSpec as P

D = 4096
LAT = 1024
TOKENS = 1280
LAYERS = 16
NX = 4
HALF = TOKENS // 2
SHARD = HALF // LAYERS
OWN = 128
WIDE = D // NX
ENC_SCALE = (LAYERS * D) ** (-0.5)
DEC_SCALE = LAT ** (-0.5)
MESSAGE = 96

bf16 = jnp.bfloat16
f32 = jnp.float32


def params(mib=48):
    return pltpu.CompilerParams(vmem_limit_bytes=mib * 1024 * 1024)


def cost(flops, nbytes):
    return pl.CostEstimate(flops=flops, bytes_accessed=nbytes, transcendentals=0)


def adam_step(weights, gradient, moment_one, moment_two):
    one_new = 0.9 * moment_one + 0.1 * gradient
    two_new = 0.999 * moment_two + 0.001 * gradient * gradient
    stepped = weights - 0.05 * one_new / (jnp.sqrt(two_new) + 1e-08)
    return (stepped, one_new, two_new)


CHUNKS = 8
CHUNK = TOKENS // CHUNKS
BLOCKS = CHUNK // SHARD


def preact_kernel(acts_ref, w_ref, dec_ref, out_ref, *rest):
    pieces, (own_ref, rows, weights, dec, row_sems, weight_sem, cut_sems, own_sems) = rest[:NX], rest[NX:]
    here, core = lax.axis_index("x"), lax.axis_index("core")
    width = pl.ds(pl.multiple_of(here * WIDE, WIDE), WIDE)
    fetch = pltpu.make_async_copy(w_ref, weights, weight_sem)
    fetch.start()

    def block(c):
        source = acts_ref.at[pl.ds(pl.multiple_of(c * CHUNK, CHUNK), CHUNK)]
        return pltpu.make_async_copy(source, rows.at[c], row_sems.at[c])

    block(0).start()
    block(1).start()
    cuts = []
    for r in range(NX):
        start = pl.multiple_of(lax.rem(here + r, NX) * WIDE, WIDE)
        cuts.append((
            pltpu.make_async_copy(dec_ref.at[:, pl.ds(start, WIDE)], dec.at[r], cut_sems.at[0, r]),
            pltpu.make_async_copy(dec.at[r], pieces[r], cut_sems.at[1, r]),
        ))
        cuts[r][0].start()

    @pl.loop(2, CHUNKS)
    def _(c):
        block(c).start()

    def own(c):
        place = lax.rem(c, CHUNKS // 2)
        target = own_ref.at[pl.ds(pl.multiple_of(place * CHUNK, CHUNK), CHUNK)]
        return pltpu.make_async_copy(rows.at[c, :, width], target, own_sems.at[place])

    def multiply(c, half):
        block(c).wait()

        @pl.when(core == half)
        def _():
            own(c).start()

        share = jnp.dot(rows[c], weights[...], preferred_element_type=f32)
        blocks = pl.ds((c - half * (CHUNKS // 2)) * BLOCKS, BLOCKS)
        out_ref[blocks, half] = (share * ENC_SCALE).reshape(BLOCKS, SHARD, OWN).astype(bf16)

    fetch.wait()

    @pl.loop(0, CHUNKS // 2)
    def _(c):
        multiply(c, 0)

    for take, give in cuts:
        take.wait()
        give.start()

    @pl.loop(CHUNKS // 2, CHUNKS)
    def _(c):
        multiply(c, 1)

    for _, give in cuts:
        give.wait()

    @pl.loop(0, CHUNKS // 2)
    def _(c):
        own(c + core * (CHUNKS // 2)).wait()


def preact_share(acts, w_enc, w_dec):
    anywhere = pl.BlockSpec(memory_space=pl.ANY)
    return pl.pallas_call(
        preact_kernel,
        in_specs=[anywhere] * 3,
        out_specs=[pl.BlockSpec(memory_space=pltpu.VMEM)] + [anywhere] * (NX + 1),
        out_shape=[jax.ShapeDtypeStruct((LAYERS, 2, SHARD, OWN), bf16)]
        + [jax.ShapeDtypeStruct((OWN, WIDE), bf16)] * NX
        + [jax.ShapeDtypeStruct((HALF, WIDE), bf16)],
        scratch_shapes=[
            pltpu.VMEM((CHUNKS, CHUNK, D), bf16),
            pltpu.VMEM((D, OWN), bf16),
            pltpu.VMEM((NX, OWN, WIDE), bf16),
            pltpu.SemaphoreType.DMA((CHUNKS,)),
            pltpu.SemaphoreType.DMA,
            pltpu.SemaphoreType.DMA((2, NX)),
            pltpu.SemaphoreType.DMA((CHUNKS // 2,)),
        ],
        compiler_params=params(60),
        cost_estimate=cost(2 * TOKENS * D * OWN, 2 * TOKENS * D),
        name="preact_share",
    )(acts, w_enc, w_dec)


def codes_kernel(got_ref, alive_ref, codes_ref, slope_ref):
    preact = jnp.sum(got_ref[...].astype(f32), axis=0)
    alive = alive_ref[...].astype(f32)
    codes_ref[...] = (alive * jax.nn.softplus(preact)).astype(bf16)
    slope_ref[...] = alive * jax.nn.sigmoid(preact)


def make_codes(got, alive):
    held = pl.BlockSpec(memory_space=pltpu.VMEM)
    return pl.pallas_call(
        codes_kernel,
        in_specs=[held] * 2,
        out_specs=[held] * 2,
        out_shape=[
            jax.ShapeDtypeStruct((2, SHARD, OWN), bf16),
            jax.ShapeDtypeStruct((2, SHARD, OWN), f32),
        ],
        compiler_params=params(16),
        cost_estimate=cost(1000000, 2000000),
        name="make_codes",
    )(got, alive)


def spread_kernel(*refs):
    out_ref = refs[NX]
    for half in range(2):
        rows = jnp.concatenate([refs[r][half].astype(f32) for r in range(NX)], axis=0).astype(bf16)
        out_ref[half] = jnp.broadcast_to(rows[None], (LAYERS, NX * SHARD, OWN))


def spread_codes(parts):
    held = pl.BlockSpec(memory_space=pltpu.VMEM)
    return pl.pallas_call(
        spread_kernel,
        in_specs=[held] * NX,
        out_specs=held,
        out_shape=jax.ShapeDtypeStruct((2, LAYERS, NX * SHARD, OWN), bf16),
        compiler_params=params(16),
        cost_estimate=cost(1000000, 2000000),
        name="spread_codes",
    )(*parts)


COLUMNS = 256


def residue_kernel(codes_ref, acts_ref, *rest):
    pieces, rest = rest[:2 * NX], rest[2 * NX:]
    share_ref, keep_ref, send_ref, got, acts, flat, cols, wide, share, halves, in_sems, out_sems = rest
    core = lax.axis_index("core")
    order = (core, 1 - core)
    fetch_codes = [pltpu.make_async_copy(codes_ref.at[order[rel]], got.at[rel], in_sems.at[rel]) for rel in range(2)]
    fetch_rest = [pltpu.make_async_copy(acts_ref, acts, in_sems.at[2])]
    for rel in range(2):
        for r in range(NX):
            rows = cols.at[rel, pl.ds(r * OWN, OWN)]
            fetch_rest.append(pltpu.make_async_copy(pieces[NX * rel + r], rows, in_sems.at[3 + NX * rel + r]))
    for copy in fetch_codes + fetch_rest:
        copy.start()
    for rel in range(2):
        fetch_codes[rel].wait()
        part = got[rel].astype(f32)
        for r in range(NX):
            rows = part[:, r * SHARD:(r + 1) * SHARD].reshape(HALF, OWN)
            flat[rel, :, r * OWN:(r + 1) * OWN] = rows.astype(bf16)
    for copy in fetch_rest:
        copy.wait()
    stores = [
        pltpu.make_async_copy(share, share_ref, out_sems.at[0]),
        pltpu.make_async_copy(halves.at[1], send_ref, out_sems.at[1]),
        pltpu.make_async_copy(halves.at[0], keep_ref, out_sems.at[2]),
    ]
    for c in range(WIDE // COLUMNS):
        block = slice(c * COLUMNS, (c + 1) * COLUMNS)
        rebuilt = jnp.dot(flat[0], cols[0, :, block], preferred_element_type=f32)
        rebuilt += jnp.dot(flat[1], cols[1, :, block], preferred_element_type=f32)
        wide[:, block] = (rebuilt * DEC_SCALE - acts[:, block].astype(f32)).astype(bf16)
    for rel in range(2):
        grad = lax.dot_general(
            wide[...], cols[rel], (((1,), (1,)), ((), ())), preferred_element_type=f32
        ) * DEC_SCALE
        parts = [grad[:, r * OWN:(r + 1) * OWN].reshape(LAYERS, SHARD, OWN) for r in range(NX)]
        share[order[rel]] = jnp.concatenate(parts, axis=1).astype(bf16)
    stores[0].start()
    for i, rel in enumerate((1, 0)):
        for c in range(WIDE // COLUMNS):
            block = slice(c * COLUMNS, (c + 1) * COLUMNS)
            grad = lax.dot_general(
                flat[rel], wide[:, block], (((0,), (0,)), ((), ())), preferred_element_type=f32
            ) * DEC_SCALE
            for r in range(NX):
                halves[rel, r, :, block] = grad[r * OWN:(r + 1) * OWN].astype(bf16)
        stores[1 + i].start()
    for copy in stores:
        copy.wait()


def residue_part(codes, acts, pieces):
    anywhere = pl.BlockSpec(memory_space=pl.ANY)
    return pl.pallas_call(
        residue_kernel,
        in_specs=[anywhere] * (2 + 2 * NX),
        out_specs=[anywhere] * 3,
        scratch_shapes=[
            pltpu.VMEM((2, LAYERS, NX * SHARD, OWN), bf16),
            pltpu.VMEM((HALF, WIDE), bf16),
            pltpu.VMEM((2, HALF, NX * OWN), bf16),
            pltpu.VMEM((2, NX * OWN, WIDE), bf16),
            pltpu.VMEM((HALF, WIDE), bf16),
            pltpu.VMEM((2, LAYERS, NX * SHARD, OWN), bf16),
            pltpu.VMEM((2, NX, OWN, WIDE), bf16),
            pltpu.SemaphoreType.DMA((3 + 2 * NX,)),
            pltpu.SemaphoreType.DMA((3,)),
        ],
        out_shape=[
            jax.ShapeDtypeStruct((2, LAYERS, NX * SHARD, OWN), bf16),
            jax.ShapeDtypeStruct((NX, OWN, WIDE), bf16),
            jax.ShapeDtypeStruct((NX, OWN, WIDE), bf16),
        ],
        compiler_params=params(60),
        cost_estimate=cost(6 * HALF * LAT * WIDE, 10000000),
        name="residue_part",
    )(codes, acts, *pieces)


def join_kernel(keep_ref, got_ref, *outs):
    for r in range(NX):
        outs[r][...] = (keep_ref[r].astype(f32) + got_ref[r].astype(f32)).astype(bf16)


def join_halves(keep, got):
    held = pl.BlockSpec(memory_space=pltpu.VMEM)
    return pl.pallas_call(
        join_kernel,
        in_specs=[held] * 2,
        out_specs=[held] * NX,
        out_shape=[jax.ShapeDtypeStruct((OWN, WIDE), bf16)] * NX,
        compiler_params=params(16),
        cost_estimate=cost(1000000, 4000000),
        name="join_halves",
    )(keep, got)


def decoder_spans(place_ref):
    return [pl.ds(pl.multiple_of(lax.rem(place_ref[1] + r, NX) * WIDE, WIDE), WIDE) for r in range(NX)]


def decoder_fetches(spans, grads, sources, taken, sems):
    fetches = []
    for r, span in enumerate(spans):
        parts = [grads[r]] + [source.at[:, span] for source in sources]
        fetches.append([pltpu.make_async_copy(part, taken.at[r, i], sems.at[r, i]) for i, part in enumerate(parts)])
    for copies in fetches:
        for copy in copies:
            copy.start()
    return fetches


def decoder_step(fetches, taken, r):
    for copy in fetches[r]:
        copy.wait()
    grad, w, m, v = (taken[r, i].astype(f32) for i in range(4))
    return adam_step(w, grad, m, v)


def size_kernel(place_ref, *refs):
    grads, (w_ref, m_ref, v_ref, rms_out) = refs[:NX], refs[NX:]
    total = jnp.zeros((OWN, OWN), f32)
    for r, span in enumerate(decoder_spans(place_ref)):
        grad, w, m, v = (part.astype(f32) for part in (grads[r][...], w_ref[:, span], m_ref[:, span], v_ref[:, span]))
        stepped = adam_step(w, grad, m, v)[0]
        square = stepped * stepped
        for c in range(WIDE // OWN):
            total += square[:, c * OWN:(c + 1) * OWN]
    rms = jnp.sqrt(jnp.sum(total.T, axis=0, keepdims=True) * (1.0 / D) + 1e-06)
    rms_out[...] = jnp.broadcast_to(rms, (8, OWN))


def decoder_size(place, grads, w, m, v):
    held = pl.BlockSpec(memory_space=pltpu.VMEM)
    return pl.pallas_call(
        size_kernel,
        in_specs=[pl.BlockSpec(memory_space=pltpu.SMEM)] + [held] * (NX + 3),
        out_specs=held,
        out_shape=jax.ShapeDtypeStruct((8, OWN), f32),
        compiler_params=params(24),
        cost_estimate=cost(20 * OWN * D, 4000000),
        name="decoder_size",
    )(place, *grads, w, m, v)


def decoder_kernel(place_ref, *refs):
    grads, (w_ref, m_ref, v_ref, *rest) = refs[:NX], refs[NX:]
    m_out, v_out, stepped_out, taken, moved, held, in_sems, out_sems = rest
    spans = decoder_spans(place_ref)
    fetches = decoder_fetches(spans, grads, (w_ref, m_ref, v_ref), taken, in_sems)
    stores = []
    for r in range(NX):
        stepped, one, two = decoder_step(fetches, taken, r)
        moved[r, 0] = one.astype(bf16)
        moved[r, 1] = two.astype(bf16)
        held[r] = stepped
        sources = (moved.at[r, 0], moved.at[r, 1], held.at[r])
        for i, target in enumerate((m_out, v_out, stepped_out)):
            stores.append(pltpu.make_async_copy(sources[i], target.at[:, spans[r]], out_sems.at[r, i]))
            stores[-1].start()
    for copy in stores:
        copy.wait()


def decoder_adam(place, grads, w, m, v):
    anywhere = pl.BlockSpec(memory_space=pl.ANY)
    return pl.pallas_call(
        decoder_kernel,
        in_specs=[pl.BlockSpec(memory_space=pltpu.SMEM)] + [anywhere] * (NX + 3),
        out_specs=[anywhere] * 3,
        out_shape=[
            jax.ShapeDtypeStruct((OWN, D), bf16),
            jax.ShapeDtypeStruct((OWN, D), bf16),
            jax.ShapeDtypeStruct((OWN, D), f32),
        ],
        scratch_shapes=[
            pltpu.VMEM((NX, 4, OWN, WIDE), bf16),
            pltpu.VMEM((NX, 2, OWN, WIDE), bf16),
            pltpu.VMEM((NX, OWN, WIDE), f32),
            pltpu.SemaphoreType.DMA((NX, 4)),
            pltpu.SemaphoreType.DMA((NX, 3)),
        ],
        compiler_params=params(54),
        cost_estimate=cost(20 * OWN * D, 8000000),
        name="decoder_adam",
    )(place, *grads, w, m, v)


def sum_kernel(got_ref, keep_ref, *outs):
    whole = jnp.sum(got_ref[...].astype(f32), axis=1)
    for r in range(NX):
        total = whole[:, r * SHARD:(r + 1) * SHARD]
        if r == 0:
            keep_ref[...] = total
        else:
            outs[r - 1][...] = total.astype(bf16)


def sum_layers(got):
    held = pl.BlockSpec(memory_space=pltpu.VMEM)
    return pl.pallas_call(
        sum_kernel,
        in_specs=[held],
        out_specs=[held] * NX,
        out_shape=[jax.ShapeDtypeStruct((2, SHARD, OWN), f32)]
        + [jax.ShapeDtypeStruct((2, SHARD, OWN), bf16)] * (NX - 1),
        compiler_params=params(16),
        cost_estimate=cost(1000000, 2000000),
        name="sum_layers",
    )(got)


def grad_pre_kernel(zero_ref, one_ref, two_ref, three_ref, slope_ref, rms_ref, out_ref):
    rms = rms_ref[...]
    high = rms.astype(bf16).astype(f32)
    mid = (rms - high).astype(bf16).astype(f32)
    low = rms - high - mid
    row = lax.broadcasted_iota(jnp.int32, (8, OWN), 0)
    tail = jnp.where(row == 0, high, jnp.where(row == 1, mid, jnp.where(row == 2, low, 0.0)))
    grad = sum(ref[...].astype(f32) for ref in (zero_ref, one_ref, two_ref, three_ref)) * slope_ref[...]
    message = jnp.concatenate([grad.reshape(2 * SHARD, OWN), tail, jnp.zeros((8, OWN), f32)], axis=0)
    out_ref[...] = jnp.broadcast_to(message.astype(bf16)[None], (LAYERS, MESSAGE, OWN))


def make_grad_pre(parts, slope, rms):
    held = pl.BlockSpec(memory_space=pltpu.VMEM)
    return pl.pallas_call(
        grad_pre_kernel,
        in_specs=[held] * 6,
        out_specs=held,
        out_shape=jax.ShapeDtypeStruct((LAYERS, MESSAGE, OWN), bf16),
        compiler_params=params(16),
        cost_estimate=cost(1000000, 2000000),
        name="make_grad_pre",
    )(*parts, slope, rms)


PART = 1024
PARTS = D // PART


def encoder_kernel(got_ref, w_ref, m_ref, v_ref, acts_ref, dec_ref, *rest):
    w_out, m_out, v_out, dec_out, acts, dec, w_new, m_new, v_new, dec_new, turned, in_sems, out_sems = rest

    def span(c):
        return pl.ds(pl.multiple_of(c * PART, PART), PART)

    def fetches(c):
        return (
            pltpu.make_async_copy(acts_ref.at[:, span(c)], acts.at[c], in_sems.at[c, 0]),
            pltpu.make_async_copy(dec_ref.at[:, span(c)], dec.at[c], in_sems.at[c, 1]),
        )

    def stores(c):
        return (
            pltpu.make_async_copy(w_new.at[c], w_out.at[span(c)], out_sems.at[c, 0]),
            pltpu.make_async_copy(m_new.at[c], m_out.at[span(c)], out_sems.at[c, 1]),
            pltpu.make_async_copy(v_new.at[c], v_out.at[span(c)], out_sems.at[c, 2]),
            pltpu.make_async_copy(dec_new.at[c], dec_out.at[:, span(c)], out_sems.at[c, 3]),
        )

    @pl.loop(0, PARTS)
    def _(c):
        for copy in fetches(c):
            copy.start()

    got = got_ref[...].astype(f32)
    for half in range(2):
        grad_pre = got[:, half * SHARD:(half + 1) * SHARD].reshape(HALF, OWN)
        turned[:, half * HALF:(half + 1) * HALF] = grad_pre.T.astype(bf16)
    rms = jnp.sum(got[:, 2 * SHARD:], axis=0)
    row = jnp.sum(rms[:3], axis=0, keepdims=True) * (1.0 / LAYERS)
    column = jnp.broadcast_to(row, (OWN, OWN)).T[:, :1]

    @pl.loop(0, PARTS)
    def _(c):
        for copy in fetches(c):
            copy.wait()
        grad = jnp.dot(turned[...], acts[c], preferred_element_type=f32) * ENC_SCALE
        grad = grad.astype(bf16).astype(f32).T
        stepped, one, two = adam_step(
            w_ref[span(c), :].astype(f32), grad, m_ref[span(c), :].astype(f32), v_ref[span(c), :].astype(f32)
        )
        w_new[c] = (stepped * row).astype(bf16)
        m_new[c] = one.astype(bf16)
        v_new[c] = two.astype(bf16)
        dec_new[c] = (dec[c] / column).astype(bf16)
        for copy in stores(c):
            copy.start()

    @pl.loop(0, PARTS)
    def _(c):
        for copy in stores(c):
            copy.wait()


def encoder_adam(got, acts, w, m, v, stepped_dec):
    held = pl.BlockSpec(memory_space=pltpu.VMEM)
    anywhere = pl.BlockSpec(memory_space=pl.ANY)
    return pl.pallas_call(
        encoder_kernel,
        in_specs=[held] * 4 + [anywhere] * 2,
        out_specs=[anywhere] * 4,
        out_shape=[jax.ShapeDtypeStruct((D, OWN), bf16)] * 3 + [jax.ShapeDtypeStruct((OWN, D), bf16)],
        scratch_shapes=[
            pltpu.VMEM((PARTS, TOKENS, PART), bf16),
            pltpu.VMEM((PARTS, OWN, PART), f32),
            pltpu.VMEM((PARTS, PART, OWN), bf16),
            pltpu.VMEM((PARTS, PART, OWN), bf16),
            pltpu.VMEM((PARTS, PART, OWN), bf16),
            pltpu.VMEM((PARTS, OWN, PART), bf16),
            pltpu.VMEM((OWN, TOKENS), bf16),
            pltpu.SemaphoreType.DMA((PARTS, 2)),
            pltpu.SemaphoreType.DMA((PARTS, 4)),
        ],
        compiler_params=params(52),
        cost_estimate=cost(2 * TOKENS * D * OWN, 20000000),
        name="encoder_adam",
    )(got, w, m, v, acts, stepped_dec)


def swap(array):
    return lax.ppermute(array, "core", [(0, 1), (1, 0)])


def shift(array, steps):
    return lax.ppermute(array, "x", [(i, (i + steps) % NX) for i in range(NX)])


def exchange(array, axes):
    flat = array.reshape(-1, array.shape[-1])
    return lax.all_to_all(flat, axes, split_axis=0, concat_axis=0, tiled=True).reshape(array.shape)


LAYER_AXES = ("y", "z")
TOKEN_AXES = ("core", "y", "z")


def local(acts, active, w_enc, m_enc, v_enc, w_dec, m_dec, v_dec):
    core = lax.axis_index("core")
    layer = lax.axis_index(LAYER_AXES)
    place = jnp.stack([core, lax.axis_index("x")]).astype(jnp.int32)
    acts, w_dec, m_dec, v_dec = (array[:, 0, :] for array in (acts, w_dec, m_dec, v_dec))

    alive = active.astype(bf16).reshape(2, LAYERS, SHARD, OWN)
    alive = lax.dynamic_index_in_dim(alive, layer, 1, keepdims=False)

    share, *mine, own_acts = preact_share(acts, w_enc[0], w_dec)
    own_cols = [mine[0]] + [shift(mine[r], r) for r in range(1, NX)]
    codes, slope = make_codes(exchange(share, LAYER_AXES), alive)
    codes = spread_codes([codes] + [shift(codes, r) for r in range(1, NX)])
    codes = exchange(codes, TOKEN_AXES)
    other_cols = [swap(piece) for piece in own_cols]
    grad_share, keep, send = residue_part(codes, own_acts, own_cols + other_cols)
    grad_share = exchange(grad_share, TOKEN_AXES)

    grad_dec = join_halves(keep, swap(send))
    grad_dec = [grad_dec[0]] + [shift(grad_dec[r], NX - r) for r in range(1, NX)]
    rms = decoder_size(place, grad_dec, w_dec, m_dec, v_dec)
    m_dec_new, v_dec_new, stepped_dec = decoder_adam(place, grad_dec, w_dec, m_dec, v_dec)

    parts = sum_layers(grad_share)
    parts = [parts[0]] + [shift(parts[r], NX - r) for r in range(1, NX)]
    messages = exchange(make_grad_pre(parts, slope, rms), LAYER_AXES)
    w_enc_new, m_enc_new, v_enc_new, w_dec_new = encoder_adam(
        messages, acts, w_enc[0], m_enc[0], v_enc[0], stepped_dec
    )
    return (
        w_enc_new[None],
        m_enc_new[None],
        v_enc_new[None],
        w_dec_new[:, None, :],
        m_dec_new[:, None, :],
        v_dec_new[:, None, :],
    )


def solution(mesh):
    fine = Mesh(mesh.devices.reshape(4, 4, NX, 2), ("y", "z", "x", "core"))
    layer = ("y", "z")
    latent = ("x", "core")
    return jax.shard_map(
        local,
        mesh=fine,
        in_specs=(
            P(None, layer, None),
            P(None, latent),
            P(layer, None, latent),
            P(layer, None, latent),
            P(layer, None, latent),
            P(latent, layer, None),
            P(latent, layer, None),
            P(latent, layer, None),
        ),
        out_specs=(
            P(layer, None, latent),
            P(layer, None, latent),
            P(layer, None, latent),
            P(latent, layer, None),
            P(latent, layer, None),
            P(latent, layer, None),
        ),
        check_vma=False,
    )
```

```python
import jax
import jax.numpy as jnp
from jax import lax
from jax.experimental import pallas as pl
from jax.experimental.pallas import tpu as pltpu
from jax.sharding import Mesh
from jax.sharding import PartitionSpec as P

D = 4096
LAT = 1024
TOKENS = 1280
LAYERS = 16
NX = 4
HALF = TOKENS // 2
SHARD = HALF // LAYERS
OWN = 128
WIDE = D // NX
ENC_SCALE = (LAYERS * D) ** (-0.5)
DEC_SCALE = LAT ** (-0.5)
MESSAGE = 96

bf16 = jnp.bfloat16
f32 = jnp.float32


def params(mib=48):
    return pltpu.CompilerParams(vmem_limit_bytes=mib * 1024 * 1024)


def cost(flops, nbytes):
    return pl.CostEstimate(flops=flops, bytes_accessed=nbytes, transcendentals=0)


def adam_step(weights, gradient, moment_one, moment_two):
    one_new = 0.9 * moment_one + 0.1 * gradient
    two_new = 0.999 * moment_two + 0.001 * gradient * gradient
    root = two_new * lax.rsqrt(two_new)
    stepped = weights - 0.05 * one_new / (root + 1e-08)
    return (stepped, one_new, two_new)


CHUNKS = 8
CHUNK = TOKENS // CHUNKS
BLOCKS = CHUNK // SHARD


def preact_kernel(acts_ref, w_ref, dec_ref, out_ref, *rest):
    pieces, (own_ref, rows, weights, dec, row_sems, weight_sem, cut_sems, own_sems) = rest[:NX], rest[NX:]
    here, core = lax.axis_index("x"), lax.axis_index("core")
    width = pl.ds(pl.multiple_of(here * WIDE, WIDE), WIDE)
    fetch = pltpu.make_async_copy(w_ref, weights, weight_sem)
    fetch.start()

    def block(c):
        source = acts_ref.at[pl.ds(pl.multiple_of(c * CHUNK, CHUNK), CHUNK)]
        return pltpu.make_async_copy(source, rows.at[c], row_sems.at[c])

    block(0).start()
    block(1).start()
    cuts = []
    for r in range(NX):
        start = pl.multiple_of(lax.rem(here + r, NX) * WIDE, WIDE)
        cuts.append((
            pltpu.make_async_copy(dec_ref.at[:, pl.ds(start, WIDE)], dec.at[r], cut_sems.at[0, r]),
            pltpu.make_async_copy(dec.at[r], pieces[r], cut_sems.at[1, r]),
        ))
        cuts[r][0].start()

    @pl.loop(2, CHUNKS)
    def _(c):
        block(c).start()

    def own(c):
        place = lax.rem(c, CHUNKS // 2)
        target = own_ref.at[pl.ds(pl.multiple_of(place * CHUNK, CHUNK), CHUNK)]
        return pltpu.make_async_copy(rows.at[c, :, width], target, own_sems.at[place])

    def multiply(c, half):
        block(c).wait()

        @pl.when(core == half)
        def _():
            own(c).start()

        share = jnp.dot(rows[c], weights[...], preferred_element_type=f32)
        blocks = pl.ds((c - half * (CHUNKS // 2)) * BLOCKS, BLOCKS)
        out_ref[blocks, half] = (share * ENC_SCALE).reshape(BLOCKS, SHARD, OWN).astype(bf16)

    fetch.wait()

    @pl.loop(0, CHUNKS // 2)
    def _(c):
        multiply(c, 0)

    for take, give in cuts:
        take.wait()
        give.start()

    @pl.loop(CHUNKS // 2, CHUNKS)
    def _(c):
        multiply(c, 1)

    for _, give in cuts:
        give.wait()

    @pl.loop(0, CHUNKS // 2)
    def _(c):
        own(c + core * (CHUNKS // 2)).wait()


def preact_share(acts, w_enc, w_dec):
    anywhere = pl.BlockSpec(memory_space=pl.ANY)
    return pl.pallas_call(
        preact_kernel,
        in_specs=[anywhere] * 3,
        out_specs=[pl.BlockSpec(memory_space=pltpu.VMEM)] + [anywhere] * (NX + 1),
        out_shape=[jax.ShapeDtypeStruct((LAYERS, 2, SHARD, OWN), bf16)]
        + [jax.ShapeDtypeStruct((OWN, WIDE), bf16)] * NX
        + [jax.ShapeDtypeStruct((HALF, WIDE), bf16)],
        scratch_shapes=[
            pltpu.VMEM((CHUNKS, CHUNK, D), bf16),
            pltpu.VMEM((D, OWN), bf16),
            pltpu.VMEM((NX, OWN, WIDE), bf16),
            pltpu.SemaphoreType.DMA((CHUNKS,)),
            pltpu.SemaphoreType.DMA,
            pltpu.SemaphoreType.DMA((2, NX)),
            pltpu.SemaphoreType.DMA((CHUNKS // 2,)),
        ],
        compiler_params=params(60),
        cost_estimate=cost(2 * TOKENS * D * OWN, 2 * TOKENS * D),
        name="preact_share",
    )(acts, w_enc, w_dec)


def codes_kernel(got_ref, alive_ref, codes_ref, slope_ref):
    preact = jnp.sum(got_ref[...].astype(f32), axis=0)
    alive = alive_ref[...].astype(f32)
    codes_ref[...] = (alive * jax.nn.softplus(preact)).astype(bf16)
    slope_ref[...] = alive * jax.nn.sigmoid(preact)


def make_codes(got, alive):
    held = pl.BlockSpec(memory_space=pltpu.VMEM)
    return pl.pallas_call(
        codes_kernel,
        in_specs=[held] * 2,
        out_specs=[held] * 2,
        out_shape=[
            jax.ShapeDtypeStruct((2, SHARD, OWN), bf16),
            jax.ShapeDtypeStruct((2, SHARD, OWN), f32),
        ],
        compiler_params=params(16),
        cost_estimate=cost(1000000, 2000000),
        name="make_codes",
    )(got, alive)


def spread_kernel(*refs):
    out_ref = refs[NX]
    for half in range(2):
        rows = jnp.concatenate([refs[r][half].astype(f32) for r in range(NX)], axis=0).astype(bf16)
        out_ref[half] = jnp.broadcast_to(rows[None], (LAYERS, NX * SHARD, OWN))


def spread_codes(parts):
    held = pl.BlockSpec(memory_space=pltpu.VMEM)
    return pl.pallas_call(
        spread_kernel,
        in_specs=[held] * NX,
        out_specs=held,
        out_shape=jax.ShapeDtypeStruct((2, LAYERS, NX * SHARD, OWN), bf16),
        compiler_params=params(16),
        cost_estimate=cost(1000000, 2000000),
        name="spread_codes",
    )(*parts)


COLUMNS = 256


def residue_kernel(codes_ref, acts_ref, *rest):
    pieces, rest = rest[:2 * NX], rest[2 * NX:]
    share_ref, keep_ref, send_ref, got, acts, flat, cols, wide, share, halves, in_sems, out_sems = rest
    core = lax.axis_index("core")
    order = (core, 1 - core)
    fetch_codes = [pltpu.make_async_copy(codes_ref.at[order[rel]], got.at[rel], in_sems.at[rel]) for rel in range(2)]
    fetch_rest = [pltpu.make_async_copy(acts_ref, acts, in_sems.at[2])]
    for rel in range(2):
        for r in range(NX):
            rows = cols.at[rel, pl.ds(r * OWN, OWN)]
            fetch_rest.append(pltpu.make_async_copy(pieces[NX * rel + r], rows, in_sems.at[3 + NX * rel + r]))
    for copy in fetch_codes + fetch_rest:
        copy.start()
    for rel in range(2):
        fetch_codes[rel].wait()
        part = got[rel].astype(f32)
        for r in range(NX):
            rows = part[:, r * SHARD:(r + 1) * SHARD].reshape(HALF, OWN)
            flat[rel, :, r * OWN:(r + 1) * OWN] = rows.astype(bf16)
    for copy in fetch_rest:
        copy.wait()
    stores = [
        pltpu.make_async_copy(share, share_ref, out_sems.at[0]),
        pltpu.make_async_copy(halves.at[1], send_ref, out_sems.at[1]),
        pltpu.make_async_copy(halves.at[0], keep_ref, out_sems.at[2]),
    ]
    for c in range(WIDE // COLUMNS):
        block = slice(c * COLUMNS, (c + 1) * COLUMNS)
        rebuilt = jnp.dot(flat[0], cols[0, :, block], preferred_element_type=f32)
        rebuilt += jnp.dot(flat[1], cols[1, :, block], preferred_element_type=f32)
        wide[:, block] = (rebuilt * DEC_SCALE - acts[:, block].astype(f32)).astype(bf16)
    for rel in range(2):
        grad = lax.dot_general(
            wide[...], cols[rel], (((1,), (1,)), ((), ())), preferred_element_type=f32
        ) * DEC_SCALE
        parts = [grad[:, r * OWN:(r + 1) * OWN].reshape(LAYERS, SHARD, OWN) for r in range(NX)]
        share[order[rel]] = jnp.concatenate(parts, axis=1).astype(bf16)
    stores[0].start()
    for i, rel in enumerate((1, 0)):
        for c in range(WIDE // COLUMNS):
            block = slice(c * COLUMNS, (c + 1) * COLUMNS)
            grad = lax.dot_general(
                flat[rel], wide[:, block], (((0,), (0,)), ((), ())), preferred_element_type=f32
            ) * DEC_SCALE
            for r in range(NX):
                halves[rel, r, :, block] = grad[r * OWN:(r + 1) * OWN].astype(bf16)
        stores[1 + i].start()
    for copy in stores:
        copy.wait()


def residue_part(codes, acts, pieces):
    anywhere = pl.BlockSpec(memory_space=pl.ANY)
    return pl.pallas_call(
        residue_kernel,
        in_specs=[anywhere] * (2 + 2 * NX),
        out_specs=[anywhere] * 3,
        scratch_shapes=[
            pltpu.VMEM((2, LAYERS, NX * SHARD, OWN), bf16),
            pltpu.VMEM((HALF, WIDE), bf16),
            pltpu.VMEM((2, HALF, NX * OWN), bf16),
            pltpu.VMEM((2, NX * OWN, WIDE), bf16),
            pltpu.VMEM((HALF, WIDE), bf16),
            pltpu.VMEM((2, LAYERS, NX * SHARD, OWN), bf16),
            pltpu.VMEM((2, NX, OWN, WIDE), bf16),
            pltpu.SemaphoreType.DMA((3 + 2 * NX,)),
            pltpu.SemaphoreType.DMA((3,)),
        ],
        out_shape=[
            jax.ShapeDtypeStruct((2, LAYERS, NX * SHARD, OWN), bf16),
            jax.ShapeDtypeStruct((NX, OWN, WIDE), bf16),
            jax.ShapeDtypeStruct((NX, OWN, WIDE), bf16),
        ],
        compiler_params=params(60),
        cost_estimate=cost(6 * HALF * LAT * WIDE, 10000000),
        name="residue_part",
    )(codes, acts, *pieces)


def join_kernel(keep_ref, got_ref, *outs):
    for r in range(NX):
        outs[r][...] = (keep_ref[r].astype(f32) + got_ref[r].astype(f32)).astype(bf16)


def join_halves(keep, got):
    held = pl.BlockSpec(memory_space=pltpu.VMEM)
    return pl.pallas_call(
        join_kernel,
        in_specs=[held] * 2,
        out_specs=[held] * NX,
        out_shape=[jax.ShapeDtypeStruct((OWN, WIDE), bf16)] * NX,
        compiler_params=params(16),
        cost_estimate=cost(1000000, 4000000),
        name="join_halves",
    )(keep, got)


def decoder_spans(place_ref):
    return [pl.ds(pl.multiple_of(lax.rem(place_ref[1] + r, NX) * WIDE, WIDE), WIDE) for r in range(NX)]


def decoder_fetches(spans, grads, sources, taken, sems):
    fetches = []
    for r, span in enumerate(spans):
        parts = [grads[r]] + [source.at[:, span] for source in sources]
        fetches.append([pltpu.make_async_copy(part, taken.at[r, i], sems.at[r, i]) for i, part in enumerate(parts)])
    for copies in fetches:
        for copy in copies:
            copy.start()
    return fetches


def decoder_step(fetches, taken, r):
    for copy in fetches[r]:
        copy.wait()
    grad, w, m, v = (taken[r, i].astype(f32) for i in range(4))
    return adam_step(w, grad, m, v)


def size_kernel(place_ref, *refs):
    grads, (w_ref, m_ref, v_ref, rms_out) = refs[:NX], refs[NX:]
    total = jnp.zeros((OWN, OWN), f32)
    for r, span in enumerate(decoder_spans(place_ref)):
        grad, w, m, v = (part.astype(f32) for part in (grads[r][...], w_ref[:, span], m_ref[:, span], v_ref[:, span]))
        stepped = adam_step(w, grad, m, v)[0]
        square = stepped * stepped
        for c in range(WIDE // OWN):
            total += square[:, c * OWN:(c + 1) * OWN]
    rms = jnp.sqrt(jnp.sum(total.T, axis=0, keepdims=True) * (1.0 / D) + 1e-06)
    rms_out[...] = jnp.broadcast_to(rms, (8, OWN))


def decoder_size(place, grads, w, m, v):
    held = pl.BlockSpec(memory_space=pltpu.VMEM)
    return pl.pallas_call(
        size_kernel,
        in_specs=[pl.BlockSpec(memory_space=pltpu.SMEM)] + [held] * (NX + 3),
        out_specs=held,
        out_shape=jax.ShapeDtypeStruct((8, OWN), f32),
        compiler_params=params(24),
        cost_estimate=cost(20 * OWN * D, 4000000),
        name="decoder_size",
    )(place, *grads, w, m, v)


def decoder_kernel(place_ref, *refs):
    grads, (w_ref, m_ref, v_ref, *rest) = refs[:NX], refs[NX:]
    m_out, v_out, stepped_out, taken, moved, held, in_sems, out_sems = rest
    spans = decoder_spans(place_ref)
    fetches = decoder_fetches(spans, grads, (w_ref, m_ref, v_ref), taken, in_sems)
    stores = []
    for r in range(NX):
        stepped, one, two = decoder_step(fetches, taken, r)
        moved[r, 0] = one.astype(bf16)
        moved[r, 1] = two.astype(bf16)
        held[r] = stepped
        sources = (moved.at[r, 0], moved.at[r, 1], held.at[r])
        for i, target in enumerate((m_out, v_out, stepped_out)):
            stores.append(pltpu.make_async_copy(sources[i], target.at[:, spans[r]], out_sems.at[r, i]))
            stores[-1].start()
    for copy in stores:
        copy.wait()


def decoder_adam(place, grads, w, m, v):
    anywhere = pl.BlockSpec(memory_space=pl.ANY)
    return pl.pallas_call(
        decoder_kernel,
        in_specs=[pl.BlockSpec(memory_space=pltpu.SMEM)] + [anywhere] * (NX + 3),
        out_specs=[anywhere] * 3,
        out_shape=[
            jax.ShapeDtypeStruct((OWN, D), bf16),
            jax.ShapeDtypeStruct((OWN, D), bf16),
            jax.ShapeDtypeStruct((OWN, D), f32),
        ],
        scratch_shapes=[
            pltpu.VMEM((NX, 4, OWN, WIDE), bf16),
            pltpu.VMEM((NX, 2, OWN, WIDE), bf16),
            pltpu.VMEM((NX, OWN, WIDE), f32),
            pltpu.SemaphoreType.DMA((NX, 4)),
            pltpu.SemaphoreType.DMA((NX, 3)),
        ],
        compiler_params=params(54),
        cost_estimate=cost(20 * OWN * D, 8000000),
        name="decoder_adam",
    )(place, *grads, w, m, v)


def sum_kernel(got_ref, keep_ref, *outs):
    whole = jnp.sum(got_ref[...].astype(f32), axis=1)
    for r in range(NX):
        total = whole[:, r * SHARD:(r + 1) * SHARD]
        if r == 0:
            keep_ref[...] = total
        else:
            outs[r - 1][...] = total.astype(bf16)


def sum_layers(got):
    held = pl.BlockSpec(memory_space=pltpu.VMEM)
    return pl.pallas_call(
        sum_kernel,
        in_specs=[held],
        out_specs=[held] * NX,
        out_shape=[jax.ShapeDtypeStruct((2, SHARD, OWN), f32)]
        + [jax.ShapeDtypeStruct((2, SHARD, OWN), bf16)] * (NX - 1),
        compiler_params=params(16),
        cost_estimate=cost(1000000, 2000000),
        name="sum_layers",
    )(got)


def grad_pre_kernel(zero_ref, one_ref, two_ref, three_ref, slope_ref, rms_ref, out_ref):
    rms = rms_ref[...]
    high = rms.astype(bf16).astype(f32)
    mid = (rms - high).astype(bf16).astype(f32)
    low = rms - high - mid
    row = lax.broadcasted_iota(jnp.int32, (8, OWN), 0)
    tail = jnp.where(row == 0, high, jnp.where(row == 1, mid, jnp.where(row == 2, low, 0.0)))
    grad = sum(ref[...].astype(f32) for ref in (zero_ref, one_ref, two_ref, three_ref)) * slope_ref[...]
    message = jnp.concatenate([grad.reshape(2 * SHARD, OWN), tail, jnp.zeros((8, OWN), f32)], axis=0)
    out_ref[...] = jnp.broadcast_to(message.astype(bf16)[None], (LAYERS, MESSAGE, OWN))


def make_grad_pre(parts, slope, rms):
    held = pl.BlockSpec(memory_space=pltpu.VMEM)
    return pl.pallas_call(
        grad_pre_kernel,
        in_specs=[held] * 6,
        out_specs=held,
        out_shape=jax.ShapeDtypeStruct((LAYERS, MESSAGE, OWN), bf16),
        compiler_params=params(16),
        cost_estimate=cost(1000000, 2000000),
        name="make_grad_pre",
    )(*parts, slope, rms)


PART = 1024
PARTS = D // PART


def encoder_kernel(got_ref, w_ref, m_ref, v_ref, acts_ref, dec_ref, *rest):
    w_out, m_out, v_out, dec_out, acts, dec, w_new, m_new, v_new, dec_new, turned, in_sems, out_sems = rest

    def span(c):
        return pl.ds(pl.multiple_of(c * PART, PART), PART)

    def fetches(c):
        return (
            pltpu.make_async_copy(acts_ref.at[:, span(c)], acts.at[c], in_sems.at[c, 0]),
            pltpu.make_async_copy(dec_ref.at[:, span(c)], dec.at[c], in_sems.at[c, 1]),
        )

    def stores(c):
        return (
            pltpu.make_async_copy(w_new.at[c], w_out.at[span(c)], out_sems.at[c, 0]),
            pltpu.make_async_copy(m_new.at[c], m_out.at[span(c)], out_sems.at[c, 1]),
            pltpu.make_async_copy(v_new.at[c], v_out.at[span(c)], out_sems.at[c, 2]),
            pltpu.make_async_copy(dec_new.at[c], dec_out.at[:, span(c)], out_sems.at[c, 3]),
        )

    @pl.loop(0, PARTS)
    def _(c):
        for copy in fetches(c):
            copy.start()

    got = got_ref[...].astype(f32)
    for half in range(2):
        grad_pre = got[:, half * SHARD:(half + 1) * SHARD].reshape(HALF, OWN)
        turned[:, half * HALF:(half + 1) * HALF] = grad_pre.T.astype(bf16)
    rms = jnp.sum(got[:, 2 * SHARD:], axis=0)
    row = jnp.sum(rms[:3], axis=0, keepdims=True) * (1.0 / LAYERS)
    column = 1.0 / jnp.broadcast_to(row, (OWN, OWN)).T[:, :1]

    @pl.loop(0, PARTS)
    def _(c):
        for copy in fetches(c):
            copy.wait()
        grad = jnp.dot(turned[...], acts[c], preferred_element_type=f32) * ENC_SCALE
        grad = grad.astype(bf16).astype(f32).T
        stepped, one, two = adam_step(
            w_ref[span(c), :].astype(f32), grad, m_ref[span(c), :].astype(f32), v_ref[span(c), :].astype(f32)
        )
        w_new[c] = (stepped * row).astype(bf16)
        m_new[c] = one.astype(bf16)
        v_new[c] = two.astype(bf16)
        dec_new[c] = (dec[c] * column).astype(bf16)
        for copy in stores(c):
            copy.start()

    @pl.loop(0, PARTS)
    def _(c):
        for copy in stores(c):
            copy.wait()


def encoder_adam(got, acts, w, m, v, stepped_dec):
    held = pl.BlockSpec(memory_space=pltpu.VMEM)
    anywhere = pl.BlockSpec(memory_space=pl.ANY)
    return pl.pallas_call(
        encoder_kernel,
        in_specs=[held] * 4 + [anywhere] * 2,
        out_specs=[anywhere] * 4,
        out_shape=[jax.ShapeDtypeStruct((D, OWN), bf16)] * 3 + [jax.ShapeDtypeStruct((OWN, D), bf16)],
        scratch_shapes=[
            pltpu.VMEM((PARTS, TOKENS, PART), bf16),
            pltpu.VMEM((PARTS, OWN, PART), f32),
            pltpu.VMEM((PARTS, PART, OWN), bf16),
            pltpu.VMEM((PARTS, PART, OWN), bf16),
            pltpu.VMEM((PARTS, PART, OWN), bf16),
            pltpu.VMEM((PARTS, OWN, PART), bf16),
            pltpu.VMEM((OWN, TOKENS), bf16),
            pltpu.SemaphoreType.DMA((PARTS, 2)),
            pltpu.SemaphoreType.DMA((PARTS, 4)),
        ],
        compiler_params=params(52),
        cost_estimate=cost(2 * TOKENS * D * OWN, 20000000),
        name="encoder_adam",
    )(got, w, m, v, acts, stepped_dec)


def swap(array):
    return lax.ppermute(array, "core", [(0, 1), (1, 0)])


def shift(array, steps):
    return lax.ppermute(array, "x", [(i, (i + steps) % NX) for i in range(NX)])


def exchange(array, axes):
    flat = array.reshape(-1, array.shape[-1])
    return lax.all_to_all(flat, axes, split_axis=0, concat_axis=0, tiled=True).reshape(array.shape)


LAYER_AXES = ("y", "z")
TOKEN_AXES = ("core", "y", "z")


def local(acts, active, w_enc, m_enc, v_enc, w_dec, m_dec, v_dec):
    core = lax.axis_index("core")
    layer = lax.axis_index(LAYER_AXES)
    place = jnp.stack([core, lax.axis_index("x")]).astype(jnp.int32)
    acts, w_dec, m_dec, v_dec = (array[:, 0, :] for array in (acts, w_dec, m_dec, v_dec))

    alive = active.astype(bf16).reshape(2, LAYERS, SHARD, OWN)
    alive = lax.dynamic_index_in_dim(alive, layer, 1, keepdims=False)

    share, *mine, own_acts = preact_share(acts, w_enc[0], w_dec)
    own_cols = [mine[0]] + [shift(mine[r], r) for r in range(1, NX)]
    codes, slope = make_codes(exchange(share, LAYER_AXES), alive)
    codes = spread_codes([codes] + [shift(codes, r) for r in range(1, NX)])
    codes = exchange(codes, TOKEN_AXES)
    other_cols = [swap(piece) for piece in own_cols]
    grad_share, keep, send = residue_part(codes, own_acts, own_cols + other_cols)
    grad_share = exchange(grad_share, TOKEN_AXES)

    grad_dec = join_halves(keep, swap(send))
    grad_dec = [grad_dec[0]] + [shift(grad_dec[r], NX - r) for r in range(1, NX)]
    rms = decoder_size(place, grad_dec, w_dec, m_dec, v_dec)
    m_dec_new, v_dec_new, stepped_dec = decoder_adam(place, grad_dec, w_dec, m_dec, v_dec)

    parts = sum_layers(grad_share)
    parts = [parts[0]] + [shift(parts[r], NX - r) for r in range(1, NX)]
    messages = exchange(make_grad_pre(parts, slope, rms), LAYER_AXES)
    w_enc_new, m_enc_new, v_enc_new, w_dec_new = encoder_adam(
        messages, acts, w_enc[0], m_enc[0], v_enc[0], stepped_dec
    )
    return (
        w_enc_new[None],
        m_enc_new[None],
        v_enc_new[None],
        w_dec_new[:, None, :],
        m_dec_new[:, None, :],
        v_dec_new[:, None, :],
    )


def solution(mesh):
    fine = Mesh(mesh.devices.reshape(4, 4, NX, 2), ("y", "z", "x", "core"))
    layer = ("y", "z")
    latent = ("x", "core")
    return jax.shard_map(
        local,
        mesh=fine,
        in_specs=(
            P(None, layer, None),
            P(None, latent),
            P(layer, None, latent),
            P(layer, None, latent),
            P(layer, None, latent),
            P(latent, layer, None),
            P(latent, layer, None),
            P(latent, layer, None),
        ),
        out_specs=(
            P(layer, None, latent),
            P(layer, None, latent),
            P(layer, None, latent),
            P(latent, layer, None),
            P(latent, layer, None),
            P(latent, layer, None),
        ),
        check_vma=False,
    )
```
